32 devices in a mesh: groups: 2 (over x), aa: 8 (over z, y), ba: 2 (over core).
Axes of the slice: x: 2, y: 2, z: 4, core: 2. Of those that a mesh axis runs over, the one named last changes fastest.
Arguments:
- video: bfloat16 [128, 8, 32, 512], P('groups', 'aa', 'ba'), parts along dimension 0, may hold values from -6 to 6
- norm_gain: float32 [3, 512], replicated, may hold values from 0.1 to 1.9
- qkv_weight: bfloat16 [3, 512, 1536], replicated, may hold values from -8 to 8
- out_weight: bfloat16 [3, 512, 512], replicated, may hold values from -0.25 to 0.25
Outputs:
- result: bfloat16 [128, 8, 32, 512], P('groups', 'aa', 'ba'), parts along dimension 0
The draws below stay inside these ranges and needn't reach their ends.
There are 2 independent parts, one for each index of `groups`. The reference program is written for one: setup_inputs(seed, part) draws one part's arguments, and reference() takes and returns one part's arrays. A program takes and returns all parts, laid end to end along the dimension named above; an argument that names none is the same for every part. Nothing has to cross between parts.
All inputs are finite; a program needn't handle non-finite values.
Results may differ from the reference program's by a relative error of at most 0.014.
Values may be sent and summed in bfloat16 or wider, within the bound.
A program may use at most 64 MiB of HBM per device.

```python
import math
import jax
import jax.numpy as jnp
from jax import lax

D = 512
HEADS = 8
HEAD_DIM = 64
BLOCKS = 3
FRAMES = 64
WIDTH = 32
HEIGHT = 8


def draw_qkv_weight(key, part):
    first_key = jax.random.fold_in(key, 0)
    drawn = jnp.clip(jax.random.normal(first_key, (BLOCKS, D, 3 * D), jnp.float32), -6.0, 6.0) * (1.0 / math.sqrt(D))
    return jnp.clip(drawn, -8.0, 8.0).astype(jnp.bfloat16)


def shard_levels(stream_key, shape, shards, smallest, largest):
    factor_of = 1.0
    for position, shards_of in shards:
        heights = jax.random.uniform(jax.random.fold_in(jax.random.fold_in(stream_key, 6), position), (shards_of,), jnp.float32, smallest / len(shards), largest / len(shards))
        factor_of = factor_of * jnp.repeat(jnp.exp(heights), shape[position] // shards_of).reshape((-1,) + (1,) * (len(shape) - 1 - position))
    return factor_of


def bell_draw(rng, dims, scale, most, cuts=(), dtype=jnp.bfloat16):
    array = scale * jax.random.normal(rng, dims, jnp.float32)
    if cuts:
        array = array * shard_levels(rng, dims, cuts, -0.22, 0.18)
    return jnp.clip(array, -most, most).astype(dtype)


def setup_inputs(seed: int = 0, part: int = 0) -> dict:
    key_list = jax.random.split(jax.random.key(seed), 5)
    part_keys = jax.random.split(jax.random.fold_in(key_list[4], part), 5)
    return {
        "video": bell_draw(part_keys[0], (FRAMES, HEIGHT, WIDTH, D), 1.0, 6.0, ((1, 8), (2, 2))),
        "norm_gain": jnp.clip(1.0 + 0.18 * jax.random.normal(key_list[1], (BLOCKS, D), jnp.float32), 0.1, 1.9),
        "qkv_weight": draw_qkv_weight(jax.random.fold_in(key_list[4], 71), part),
        "out_weight": bell_draw(key_list[3], (BLOCKS, D, D), D ** -0.5, 0.25),
    }


score_forms = ('sbcnd,tbcnd->bcnst', 'ascnd,atcnd->acnst', 'absnd,abtnd->abnst')
mix_forms = ('bcnst,tbcnd->sbcnd', 'acnst,atcnd->ascnd', 'abnst,abtnd->absnd')

def attend(queries, key_rows, value_rows, line):
    shape = queries.shape
    split = shape[:3] + (HEADS, HEAD_DIM)
    scores = jnp.einsum(score_forms[line], queries.reshape(split).astype(jnp.float32), key_rows.reshape(split).astype(jnp.float32)) * (1.0 / math.sqrt(HEAD_DIM))
    weights = jax.nn.softmax(scores, axis=-1).astype(jnp.bfloat16)
    mixed = jnp.einsum(mix_forms[line], weights.astype(jnp.float32), value_rows.reshape(split).astype(jnp.float32))
    return mixed.astype(jnp.bfloat16).reshape(shape)

def full_block(state, gain, weight_in, weight_out, line):
    floats = state.astype(jnp.float32)
    meansq = lax.optimization_barrier(jnp.mean(floats * floats, axis=-1, keepdims=True))
    normed = (floats * lax.rsqrt(meansq + 1e-06) * gain).astype(jnp.bfloat16)
    packed = jnp.dot(normed, weight_in, preferred_element_type=jnp.float32).astype(jnp.bfloat16)
    width = state.shape[-1]
    mixed = attend(packed[..., :width], packed[..., width:2 * width], packed[..., 2 * width:], line)
    update = jnp.dot(mixed, weight_out, preferred_element_type=jnp.float32)
    return (floats + update).astype(jnp.bfloat16)

def reference(video, norm_gain, qkv_weight, out_weight):
    by_row = jnp.moveaxis(video, 1, 0)
    by_row = lax.map(lambda plane: full_block(plane[None], norm_gain[0], qkv_weight[0], out_weight[0], 1)[0], by_row)
    state = jnp.moveaxis(by_row, 0, 1)
    state = lax.map(lambda plane: full_block(plane[None], norm_gain[1], qkv_weight[1], out_weight[1], 1)[0], state)
    state = lax.map(lambda plane: full_block(plane[None], norm_gain[2], qkv_weight[2], out_weight[2], 2)[0], state)
    return state
```

```python
import functools
import math

import jax
import jax.numpy as jnp
from jax import lax
from jax.experimental import pallas as pl
from jax.experimental.pallas import tpu as pltpu
from jax.sharding import PartitionSpec as P

HEADS = 8
HEAD_DIM = 64
PIECE = 16
GROUP = 128
LANES = 128
MESH = pl.DeviceIdType.MESH


score_forms = ("sbcnd,tbcnd->bcnst", "ascnd,atcnd->acnst", "absnd,abtnd->abnst")
mix_forms = ("bcnst,tbcnd->sbcnd", "acnst,atcnd->ascnd", "abnst,abtnd->absnd")


def attend(queries, key_rows, value_rows, line):
    shape = queries.shape
    split = shape[:3] + (HEADS, HEAD_DIM)
    scores = jnp.einsum(
        score_forms[line],
        queries.reshape(split),
        key_rows.reshape(split),
        preferred_element_type=jnp.float32,
    ) * (1.0 / math.sqrt(HEAD_DIM))
    weights = jax.nn.softmax(scores, axis=-1).astype(jnp.bfloat16)
    mixed = jnp.einsum(
        mix_forms[line], weights, value_rows.reshape(split), preferred_element_type=jnp.float32
    )
    return mixed.astype(jnp.bfloat16).reshape(shape)


def full_block(state, gain, weight_in, weight_out, line):
    floats = state.astype(jnp.float32)
    meansq = jnp.mean(floats * floats, axis=-1, keepdims=True)
    normed = (floats * lax.rsqrt(meansq + 1e-06) * gain).astype(jnp.bfloat16)
    packed = jnp.dot(normed, weight_in, preferred_element_type=jnp.float32).astype(jnp.bfloat16)
    width = state.shape[-1]
    mixed = attend(packed[..., :width], packed[..., width : 2 * width], packed[..., 2 * width :], line)
    update = jnp.dot(mixed, weight_out, preferred_element_type=jnp.float32)
    return (floats + update).astype(jnp.bfloat16)


def general_body(video, norm_gain, qkv_weight, out_weight):
    state = full_block(video, norm_gain[0], qkv_weight[0], out_weight[0], 0)
    state = lax.all_to_all(state, "aa", split_axis=0, concat_axis=1, tiled=True)
    state = full_block(state, norm_gain[1], qkv_weight[1], out_weight[1], 1)
    state = lax.all_to_all(state, "ba", split_axis=1, concat_axis=2, tiled=True)
    state = full_block(state, norm_gain[2], qkv_weight[2], out_weight[2], 2)
    state = lax.all_to_all(state, "ba", split_axis=2, concat_axis=1, tiled=True)
    return lax.all_to_all(state, "aa", split_axis=1, concat_axis=0, tiled=True)


def block_on(x, gain, w_in, w_out, line_of):
    tokens, d = x.shape
    meansq = jnp.mean(x * x, axis=-1, keepdims=True)
    normed = (x * lax.rsqrt(meansq + 1e-06) * gain).astype(jnp.bfloat16)
    packed = jnp.dot(normed, w_in, preferred_element_type=jnp.float32)

    pair = 2 * HEAD_DIM
    lane = lax.broadcasted_iota(jnp.int32, (GROUP, pair), 1)
    low = lane < HEAD_DIM
    scale = 1.0 / math.sqrt(HEAD_DIM)
    keep_low = jnp.where(low, scale, 0.0)
    keep_high = jnp.where(low, 0.0, scale)
    rows = line_of(lax.broadcasted_iota(jnp.int32, (2 * GROUP, GROUP), 0) % GROUP)
    cols = line_of(lax.broadcasted_iota(jnp.int32, (2 * GROUP, GROUP), 1))
    bias = jnp.where(rows == cols, 0.0, -jnp.inf)
    ones = jnp.ones((GROUP, pair), jnp.bfloat16)

    groups = []
    for g in range(tokens // GROUP):
        at = slice(g * GROUP, (g + 1) * GROUP)
        heads = []
        for p in range(d // pair):
            q = packed[at, p * pair : (p + 1) * pair]
            k = packed[at, d + p * pair : d + (p + 1) * pair].astype(jnp.bfloat16)
            v = packed[at, 2 * d + p * pair : 2 * d + (p + 1) * pair].astype(jnp.bfloat16)
            q2 = jnp.concatenate([q * keep_low, q * keep_high], axis=0).astype(jnp.bfloat16)
            s = lax.dot_general(q2, k, (((1,), (1,)), ((), ())), preferred_element_type=jnp.float32)
            s = s + bias
            e = jnp.exp(s - jnp.max(s, axis=-1, keepdims=True)).astype(jnp.bfloat16)
            o = jnp.dot(e, jnp.concatenate([v, ones], axis=1), preferred_element_type=jnp.float32)
            o = o[:, :pair] / o[:, pair:]
            heads.append(jnp.where(low, o[:GROUP], o[GROUP:]))
        groups.append(jnp.concatenate(heads, axis=1))
    mixed = jnp.concatenate(groups, axis=0).astype(jnp.bfloat16)
    return x + jnp.dot(mixed, w_out, preferred_element_type=jnp.float32)


def load_strided(ref, start, size, stride):
    return jnp.concatenate(
        [ref[p, pl.ds(start, size, stride=stride), :] for p in range(ref.shape[0])], axis=1
    )


def kernel(
    sizes, gain_ref, x_hbm, wi_hbm, wo_hbm, out_ref,
    x_ref, wi_ref, wo_ref, x32, turned, send, recv, y1, back,
    x_sem, w_sem, send_sem, recv_sem, back_sem, out_sem, own_sem,
):
    frames, rows, cols, n, cores = sizes
    mine = frames // n
    wide = PIECE // mine
    chunks = cols // wide
    per_group = GROUP // frames
    d = x_ref.shape[-1]
    planes = d // LANES
    aa, ba = lax.axis_index("aa"), lax.axis_index("ba")
    me = aa * cores + ba

    copies = [pltpu.make_async_copy(x_hbm, x_ref, x_sem)]
    for b in range(3):
        copies.append(pltpu.make_async_copy(wi_hbm.at[b], wi_ref.at[b], w_sem.at[b, 0]))
        copies.append(pltpu.make_async_copy(wo_hbm.at[b], wo_ref.at[b], w_sem.at[b, 1]))
    for copy in copies:
        copy.start()

    def where(device):
        return {"aa": device // cores, "ba": device % cores}

    barrier = pltpu.get_barrier_semaphore()

    def greet(o, c):
        pl.semaphore_signal(
            barrier, inc=1, device_id=where(lax.rem(me + o, n)), device_id_type=MESH
        )
        return c

    lax.fori_loop(1, n, greet, 0)
    copies[0].wait()
    for p in range(planes):
        x32[p] = x_ref[:, p * LANES : (p + 1) * LANES].astype(jnp.float32)
    pl.semaphore_wait(barrier, n - 1)

    copies[1].wait()
    copies[2].wait()

    def first(k, c):
        spots = [(w, f) for w in range(wide) for f in range(mine)]
        x = jnp.concatenate(
            [load_strided(x32, f * cols + k * wide + w, n, mine * cols) for w, f in spots], axis=0
        )
        y = block_on(x, gain_ref[0:1, :], wi_ref[0], wo_ref[0], lambda i: i // frames)
        for at, (w, f) in enumerate(spots):
            for p in range(planes):
                turned[p, pl.ds(w * mine + f, n, stride=PIECE), :] = y[
                    at * n : (at + 1) * n, p * LANES : (p + 1) * LANES
                ]
        for p in range(planes):
            send[k, :, :, p * LANES : (p + 1) * LANES] = (
                turned[p].astype(jnp.bfloat16).reshape(n, PIECE, LANES)
            )
        recv[k, ba, aa] = send[k, me]

        def give(o, c):
            device = lax.rem(me + o, n)
            pltpu.make_async_remote_copy(
                src_ref=send.at[k, device], dst_ref=recv.at[k, ba, aa],
                send_sem=send_sem, recv_sem=recv_sem.at[k],
                device_id=where(device), device_id_type=MESH,
            ).start()
            return c

        lax.fori_loop(1, n, give, 0)
        return c

    lax.fori_loop(0, chunks, first, 0)

    copies[3].wait()
    copies[4].wait()

    def second(k, c):
        pltpu.make_async_copy(send.at[0, 0 : n - 1], send.at[0, 0 : n - 1], recv_sem.at[k]).wait()
        x = recv[k].reshape(n * PIECE, d).astype(jnp.float32)
        y = block_on(x, gain_ref[1:2, :], wi_ref[1], wo_ref[1], lambda i: i % PIECE)
        for at in range(n):
            place = pl.multiple_of((at * chunks + k) * PIECE, PIECE)
            for p in range(planes):
                y1[p, pl.ds(place, PIECE), :] = y[
                    at * PIECE : (at + 1) * PIECE, p * LANES : (p + 1) * LANES
                ]
        return c

    lax.fori_loop(0, chunks, second, 0)

    copies[5].wait()
    copies[6].wait()
    some = GROUP // (cores * cols)

    def third(f, c):
        parts = [
            load_strided(y1, (b * rows + r) * cols * mine + f, some * cols, mine)
            for r in range(0, rows, some)
            for b in range(cores)
        ]
        x = jnp.concatenate(parts, axis=0)
        y = block_on(x, gain_ref[2:3, :], wi_ref[2], wo_ref[2], lambda i: (i // cols) % some)
        back[f] = y.astype(jnp.bfloat16).reshape(n, cols, d)
        frame = me * mine + f

        def place(device):
            r, b = device // cores, device % cores
            return ((r // some) * cores + b) * some + r % some

        pltpu.make_async_copy(
            back.at[f, place(me)], out_ref.at[frame], own_sem.at[f]
        ).start()

        def give(o, c):
            device = lax.rem(me + o, n)
            pltpu.make_async_remote_copy(
                src_ref=back.at[f, place(device)], dst_ref=out_ref.at[frame],
                send_sem=back_sem, recv_sem=out_sem,
                device_id=where(device), device_id_type=MESH,
            ).start()
            return c

        lax.fori_loop(1, n, give, 0)
        return c

    lax.fori_loop(0, mine, third, 0)

    for f in range(mine):
        pltpu.make_async_copy(back.at[f, 0], out_ref.at[f], own_sem.at[f]).wait()
    for sem, buffer in ((send_sem, send), (back_sem, back)):
        pltpu.make_async_copy(
            buffer.at[:, 0 : n - 1], buffer.at[:, 0 : n - 1], sem
        ).wait()
    others = (n - 1) * mine
    pltpu.make_async_copy(out_ref.at[0:others], out_ref.at[0:others], out_sem).wait()


def kernel_body(sizes, video, norm_gain, qkv_weight, out_weight):
    frames, rows, cols, n, cores = sizes
    d = video.shape[-1]
    tokens = frames * cols
    planes = d // LANES
    mine = frames // n
    chunks = cols * mine // PIECE
    dma = pltpu.SemaphoreType.DMA
    result = pl.pallas_call(
        functools.partial(kernel, sizes),
        out_shape=jax.ShapeDtypeStruct((frames, cols, d), jnp.bfloat16),
        in_specs=[pl.BlockSpec(memory_space=pltpu.VMEM)] + [pl.BlockSpec(memory_space=pl.ANY)] * 3,
        out_specs=pl.BlockSpec(memory_space=pl.ANY),
        scratch_shapes=[
            pltpu.VMEM((tokens, d), jnp.bfloat16),
            pltpu.VMEM(qkv_weight.shape, jnp.bfloat16),
            pltpu.VMEM(out_weight.shape, jnp.bfloat16),
            pltpu.VMEM((planes, tokens, LANES), jnp.float32),
            pltpu.VMEM((planes, n * PIECE, LANES), jnp.float32),
            pltpu.VMEM((chunks, n, PIECE, d), jnp.bfloat16),
            pltpu.VMEM((chunks, cores, n // cores, PIECE, d), jnp.bfloat16),
            pltpu.VMEM((planes, tokens, LANES), jnp.float32),
            pltpu.VMEM((mine, n, cols, d), jnp.bfloat16),
            dma,
            dma((3, 2)),
            dma,
            dma((chunks,)),
            dma,
            dma,
            dma((mine,)),
        ],
        compiler_params=pltpu.CompilerParams(
            collective_id=0, has_side_effects=True, vmem_limit_bytes=48 * 1024 * 1024
        ),
        cost_estimate=pl.CostEstimate(
            flops=2 * tokens * d * 4 * d * 3, bytes_accessed=8 * tokens * d, transcendentals=0
        ),
    )(norm_gain, video.reshape(tokens, d), qkv_weight, out_weight)
    return result.reshape(video.shape)


def fits(frames, rows, cols, n, cores, d):
    if frames % n or n != rows * cores or d % (2 * HEAD_DIM):
        return False
    mine = frames // n
    if PIECE % mine or cols != PIECE or GROUP % frames or rows * PIECE != GROUP:
        return False
    return GROUP % (cores * cols) == 0 and (n * PIECE) % GROUP == 0


def solution(mesh):
    def body(video, norm_gain, qkv_weight, out_weight):
        frames, here, cols, d = video.shape
        cores = mesh.shape["ba"]
        rows = here * mesh.shape["aa"]
        n = mesh.shape["aa"] * cores
        if here == 1 and fits(frames, rows, cols, n, cores, d):
            sizes = (frames, rows, cols, n, cores)
            return kernel_body(sizes, video, norm_gain, qkv_weight, out_weight)
        return general_body(video, norm_gain, qkv_weight, out_weight)

    return jax.shard_map(
        body,
        mesh=mesh,
        in_specs=(P("groups", "aa", "ba", None), P(), P(), P()),
        out_specs=P("groups", "aa", "ba", None),
        check_vma=False,
    )
```

```python
import functools
import math

import jax
import jax.numpy as jnp
from jax import lax
from jax.experimental import pallas as pl
from jax.experimental.pallas import tpu as pltpu
from jax.sharding import PartitionSpec as P

HEADS = 8
HEAD_DIM = 64
PIECE = 16
GROUP = 128
LANES = 128
MESH = pl.DeviceIdType.MESH


score_forms = ("sbcnd,tbcnd->bcnst", "ascnd,atcnd->acnst", "absnd,abtnd->abnst")
mix_forms = ("bcnst,tbcnd->sbcnd", "acnst,atcnd->ascnd", "abnst,abtnd->absnd")


def attend(queries, key_rows, value_rows, line):
    shape = queries.shape
    split = shape[:3] + (HEADS, HEAD_DIM)
    scores = jnp.einsum(
        score_forms[line],
        queries.reshape(split),
        key_rows.reshape(split),
        preferred_element_type=jnp.float32,
    ) * (1.0 / math.sqrt(HEAD_DIM))
    weights = jax.nn.softmax(scores, axis=-1).astype(jnp.bfloat16)
    mixed = jnp.einsum(
        mix_forms[line], weights, value_rows.reshape(split), preferred_element_type=jnp.float32
    )
    return mixed.astype(jnp.bfloat16).reshape(shape)


def full_block(state, gain, weight_in, weight_out, line):
    floats = state.astype(jnp.float32)
    meansq = jnp.mean(floats * floats, axis=-1, keepdims=True)
    normed = (floats * lax.rsqrt(meansq + 1e-06) * gain).astype(jnp.bfloat16)
    packed = jnp.dot(normed, weight_in, preferred_element_type=jnp.float32).astype(jnp.bfloat16)
    width = state.shape[-1]
    mixed = attend(packed[..., :width], packed[..., width : 2 * width], packed[..., 2 * width :], line)
    update = jnp.dot(mixed, weight_out, preferred_element_type=jnp.float32)
    return (floats + update).astype(jnp.bfloat16)


def general_body(video, norm_gain, qkv_weight, out_weight):
    state = full_block(video, norm_gain[0], qkv_weight[0], out_weight[0], 0)
    state = lax.all_to_all(state, "aa", split_axis=0, concat_axis=1, tiled=True)
    state = full_block(state, norm_gain[1], qkv_weight[1], out_weight[1], 1)
    state = lax.all_to_all(state, "ba", split_axis=1, concat_axis=2, tiled=True)
    state = full_block(state, norm_gain[2], qkv_weight[2], out_weight[2], 2)
    state = lax.all_to_all(state, "ba", split_axis=2, concat_axis=1, tiled=True)
    return lax.all_to_all(state, "aa", split_axis=1, concat_axis=0, tiled=True)


def block_on(x, gain, w_in, w_out, line_of):
    tokens, d = x.shape
    meansq = jnp.mean(x * x, axis=-1, keepdims=True)
    normed = (x * lax.rsqrt(meansq + 1e-06) * gain).astype(jnp.bfloat16)
    packed = jnp.dot(normed, w_in, preferred_element_type=jnp.float32)

    pair = 2 * HEAD_DIM
    lane = lax.broadcasted_iota(jnp.int32, (GROUP, pair), 1)
    low = lane < HEAD_DIM
    scale = 1.0 / math.sqrt(HEAD_DIM)
    keep_low = jnp.where(low, scale, 0.0)
    keep_high = jnp.where(low, 0.0, scale)
    rows = line_of(lax.broadcasted_iota(jnp.int32, (2 * GROUP, GROUP), 0) % GROUP)
    cols = line_of(lax.broadcasted_iota(jnp.int32, (2 * GROUP, GROUP), 1))
    bias = jnp.where(rows == cols, 0.0, -jnp.inf)
    ones = jnp.ones((GROUP, pair), jnp.bfloat16)

    groups = []
    for g in range(tokens // GROUP):
        at = slice(g * GROUP, (g + 1) * GROUP)
        heads = []
        for p in range(d // pair):
            q = packed[at, p * pair : (p + 1) * pair]
            k = packed[at, d + p * pair : d + (p + 1) * pair].astype(jnp.bfloat16)
            v = packed[at, 2 * d + p * pair : 2 * d + (p + 1) * pair].astype(jnp.bfloat16)
            q2 = jnp.concatenate([q * keep_low, q * keep_high], axis=0).astype(jnp.bfloat16)
            s = lax.dot_general(q2, k, (((1,), (1,)), ((), ())), preferred_element_type=jnp.float32)
            s = s + bias
            e = jnp.exp(s - jnp.max(s, axis=-1, keepdims=True)).astype(jnp.bfloat16)
            o = jnp.dot(e, jnp.concatenate([v, ones], axis=1), preferred_element_type=jnp.float32)
            o = o[:, :pair] / o[:, pair:]
            heads.append(jnp.where(low, o[:GROUP], o[GROUP:]))
        groups.append(jnp.concatenate(heads, axis=1))
    mixed = jnp.concatenate(groups, axis=0).astype(jnp.bfloat16)
    return x + jnp.dot(mixed, w_out, preferred_element_type=jnp.float32)


def load_strided(ref, start, size, stride):
    return jnp.concatenate(
        [ref[p, pl.ds(start, size, stride=stride), :] for p in range(ref.shape[0])], axis=1
    )


def kernel(
    sizes, gain_hbm, x_hbm, wi_hbm, wo_hbm, out_ref,
    gain_ref, x_ref, wi_ref, wo_ref, x32, turned, late, send, recv, y1, y1_late, back,
    x_sem, w_sem, send_sem, recv_sem, back_sem, out_sem, own_sem,
):
    frames, rows, cols, n, cores = sizes
    mine = frames // n
    wide = PIECE // mine
    half = cols // 2
    early = half // wide
    few = PIECE // half
    d = x_ref.shape[-1]
    planes = d // LANES
    aa, ba = lax.axis_index("aa"), lax.axis_index("ba")
    me = aa * cores + ba

    x_copies = [
        pltpu.make_async_copy(x_hbm, x_ref, x_sem.at[0]),
        pltpu.make_async_copy(gain_hbm, gain_ref, x_sem.at[1]),
    ]
    w_copies = []
    for b in range(3):
        w_copies.append(pltpu.make_async_copy(wi_hbm.at[b], wi_ref.at[b], w_sem.at[b, 0]))
        w_copies.append(pltpu.make_async_copy(wo_hbm.at[b], wo_ref.at[b], w_sem.at[b, 1]))
    for copy in x_copies + w_copies[:2]:
        copy.start()

    def where(device):
        return {"aa": device // cores, "ba": device % cores}

    near = n // 2

    def other(o):
        side = me // near
        side = jnp.where(o < near, 1 - side, side)
        return side * near + lax.rem(me + o, near)

    barrier = pltpu.get_barrier_semaphore()

    def greet(o, c):
        pl.semaphore_signal(barrier, inc=1, device_id=where(other(o)), device_id_type=MESH)
        return c

    def others(body):
        def step(i, c):
            return body(jnp.where(i < near, i, i + 1), c)

        lax.fori_loop(0, n - 1, step, 0)

    others(greet)
    for copy in x_copies:
        copy.wait()
    for p in range(planes):
        x32[p] = x_ref[:, p * LANES : (p + 1) * LANES].astype(jnp.float32)
    for copy in w_copies[:2]:
        copy.wait()
    for copy in w_copies[2:]:
        copy.start()
    pl.semaphore_wait(barrier, n - 1)

    spots = [(w, f) for w in range(wide) for f in range(mine)]

    def along_frames(k):
        x = jnp.concatenate(
            [load_strided(x32, f * cols + k * wide + w, n, mine * cols) for w, f in spots], axis=0
        )
        return block_on(x, gain_ref[0:1, :], wi_ref[0], wo_ref[0], lambda i: i // frames)

    def give_chunk(k):
        recv[k, ba, aa] = send[k, me]

        def give(o, c):
            device = other(o)
            pltpu.make_async_remote_copy(
                src_ref=send.at[k, device], dst_ref=recv.at[k, ba, aa],
                send_sem=send_sem, recv_sem=recv_sem.at[k],
                device_id=where(device), device_id_type=MESH,
            ).start()
            return c

        others(give)

    def first(k, c):
        y = along_frames(k)
        for at, (w, f) in enumerate(spots):
            for p in range(planes):
                turned[p, pl.ds(w * mine + f, n, stride=PIECE), :] = y[
                    at * n : (at + 1) * n, p * LANES : (p + 1) * LANES
                ]
        for p in range(planes):
            send[k, :, :, p * LANES : (p + 1) * LANES] = (
                turned[p].astype(jnp.bfloat16).reshape(n, PIECE, LANES)
            )
        give_chunk(k)
        return c

    lax.fori_loop(0, early, first, 0)

    def first_late(k, c):
        y = along_frames(early + k)
        for at, (w, f) in enumerate(spots):
            row = (f // few) * n * PIECE + (k * wide + w) * few + f % few
            for p in range(planes):
                late[p, pl.ds(row, n, stride=PIECE), :] = y[
                    at * n : (at + 1) * n, p * LANES : (p + 1) * LANES
                ]
        return c

    lax.fori_loop(0, early, first_late, 0)
    for h in range(mine // few):
        for p in range(planes):
            send[early + h, :, :, p * LANES : (p + 1) * LANES] = (
                late[p, h * n * PIECE : (h + 1) * n * PIECE]
                .astype(jnp.bfloat16)
                .reshape(n, PIECE, LANES)
            )
        give_chunk(early + h)

    for copy in w_copies[2:]:
        copy.wait()

    def along_rows(k):
        pltpu.make_async_copy(send.at[0, 0 : n - 1], send.at[0, 0 : n - 1], recv_sem.at[k]).wait()
        x = recv[k].reshape(n * PIECE, d).astype(jnp.float32)
        return block_on(x, gain_ref[1:2, :], wi_ref[1], wo_ref[1], lambda i: i % PIECE)

    def second(k, c):
        y = along_rows(k)
        for at in range(n):
            place = pl.multiple_of((at * early + k) * PIECE, PIECE)
            for p in range(planes):
                y1[p, pl.ds(place, PIECE), :] = y[
                    at * PIECE : (at + 1) * PIECE, p * LANES : (p + 1) * LANES
                ]
        return c

    lax.fori_loop(0, early, second, 0)

    some = GROUP // (cores * cols)

    def third(h, i):
        f = h * few + i
        parts = []
        for r in range(0, rows, some):
            for b in range(cores):
                at = b * rows + r
                parts.append(load_strided(y1, at * half * mine + f, some * half, mine))
                parts.append(load_strided(y1_late, at * half * few + i, some * half, few))
        x = jnp.concatenate(parts, axis=0)
        y = block_on(x, gain_ref[2:3, :], wi_ref[2], wo_ref[2], lambda t: (t // half) % some)
        for at in range(n):
            low = (at // some) * 2 * some * half + (at % some) * half
            high = low + some * half
            piece = jnp.concatenate([y[low : low + half], y[high : high + half]], axis=0)
            back[f, at] = piece.astype(jnp.bfloat16)
        frame = me * mine + f

        def place(device):
            r, b = device // cores, device % cores
            return ((r // some) * cores + b) * some + r % some

        pltpu.make_async_copy(
            back.at[f, place(me)], out_ref.at[frame], own_sem.at[f]
        ).start()

        def give(o, c):
            device = other(o)
            pltpu.make_async_remote_copy(
                src_ref=back.at[f, place(device)], dst_ref=out_ref.at[frame],
                send_sem=back_sem, recv_sem=out_sem,
                device_id=where(device), device_id_type=MESH,
            ).start()
            return c

        others(give)

    def rest(h, c):
        y = along_rows(early + h)
        for p in range(planes):
            y1_late[p] = y[:, p * LANES : (p + 1) * LANES]

        def frame_of(i, c):
            third(h, i)
            return c

        return lax.fori_loop(0, few, frame_of, c)

    lax.fori_loop(0, mine // few, rest, 0)

    for f in range(mine):
        pltpu.make_async_copy(back.at[f, 0], out_ref.at[f], own_sem.at[f]).wait()
    for sem, buffer in ((send_sem, send), (back_sem, back)):
        pltpu.make_async_copy(
            buffer.at[:, 0 : n - 1], buffer.at[:, 0 : n - 1], sem
        ).wait()
    total = (n - 1) * mine
    pltpu.make_async_copy(out_ref.at[0:total], out_ref.at[0:total], out_sem).wait()


def kernel_body(sizes, video, norm_gain, qkv_weight, out_weight):
    frames, rows, cols, n, cores = sizes
    d = video.shape[-1]
    tokens = frames * cols
    planes = d // LANES
    mine = frames // n
    chunks = cols * mine // PIECE
    dma = pltpu.SemaphoreType.DMA
    result = pl.pallas_call(
        functools.partial(kernel, sizes),
        out_shape=jax.ShapeDtypeStruct((frames, cols, d), jnp.bfloat16),
        in_specs=[pl.BlockSpec(memory_space=pltpu.HBM)] * 4,
        out_specs=pl.BlockSpec(memory_space=pl.ANY),
        scratch_shapes=[
            pltpu.VMEM(norm_gain.shape, jnp.float32),
            pltpu.VMEM((tokens, d), jnp.bfloat16),
            pltpu.VMEM(qkv_weight.shape, jnp.bfloat16),
            pltpu.VMEM(out_weight.shape, jnp.bfloat16),
            pltpu.VMEM((planes, tokens, LANES), jnp.float32),
            pltpu.VMEM((planes, n * PIECE, LANES), jnp.float32),
            pltpu.VMEM((planes, tokens // 2, LANES), jnp.float32),
            pltpu.VMEM((chunks, n, PIECE, d), jnp.bfloat16),
            pltpu.VMEM((chunks, cores, n // cores, PIECE, d), jnp.bfloat16),
            pltpu.VMEM((planes, tokens // 2, LANES), jnp.float32),
            pltpu.VMEM((planes, n * PIECE, LANES), jnp.float32),
            pltpu.VMEM((mine, n, cols, d), jnp.bfloat16),
            dma((2,)),
            dma((3, 2)),
            dma,
            dma((chunks,)),
            dma,
            dma,
            dma((mine,)),
        ],
        compiler_params=pltpu.CompilerParams(
            collective_id=0, has_side_effects=True, vmem_limit_bytes=62 * 1024 * 1024
        ),
        cost_estimate=pl.CostEstimate(
            flops=2 * tokens * d * 4 * d * 3, bytes_accessed=8 * tokens * d, transcendentals=0
        ),
    )(norm_gain, video.reshape(tokens, d), qkv_weight, out_weight)
    return result.reshape(video.shape)


def fits(frames, rows, cols, n, cores, d):
    if frames % n or n != rows * cores or n % 2 or d % (2 * HEAD_DIM):
        return False
    mine = frames // n
    if PIECE % mine or cols != PIECE or GROUP % frames or rows * PIECE != GROUP:
        return False
    half = cols // 2
    if half % (PIECE // mine) or mine % (PIECE // half):
        return False
    return GROUP % (cores * cols) == 0 and (n * PIECE) % GROUP == 0


def solution(mesh):
    def body(video, norm_gain, qkv_weight, out_weight):
        frames, here, cols, d = video.shape
        cores = mesh.shape["ba"]
        rows = here * mesh.shape["aa"]
        n = mesh.shape["aa"] * cores
        if here == 1 and fits(frames, rows, cols, n, cores, d):
            sizes = (frames, rows, cols, n, cores)
            return kernel_body(sizes, video, norm_gain, qkv_weight, out_weight)
        return general_body(video, norm_gain, qkv_weight, out_weight)

    return jax.shard_map(
        body,
        mesh=mesh,
        in_specs=(P("groups", "aa", "ba", None), P(), P(), P()),
        out_specs=P("groups", "aa", "ba", None),
        check_vma=False,
    )
```

```python
import functools
import math

import jax
import jax.numpy as jnp
from jax import lax
from jax.experimental import pallas as pl
from jax.experimental.pallas import tpu as pltpu
from jax.sharding import PartitionSpec as P

HEADS = 8
HEAD_DIM = 64
PIECE = 16
GROUP = 128
LANES = 128
MESH = pl.DeviceIdType.MESH


score_forms = ("sbcnd,tbcnd->bcnst", "ascnd,atcnd->acnst", "absnd,abtnd->abnst")
mix_forms = ("bcnst,tbcnd->sbcnd", "acnst,atcnd->ascnd", "abnst,abtnd->absnd")


def attend(queries, key_rows, value_rows, line):
    shape = queries.shape
    split = shape[:3] + (HEADS, HEAD_DIM)
    scores = jnp.einsum(
        score_forms[line],
        queries.reshape(split),
        key_rows.reshape(split),
        preferred_element_type=jnp.float32,
    ) * (1.0 / math.sqrt(HEAD_DIM))
    weights = jax.nn.softmax(scores, axis=-1).astype(jnp.bfloat16)
    mixed = jnp.einsum(
        mix_forms[line], weights, value_rows.reshape(split), preferred_element_type=jnp.float32
    )
    return mixed.astype(jnp.bfloat16).reshape(shape)


def full_block(state, gain, weight_in, weight_out, line):
    floats = state.astype(jnp.float32)
    meansq = jnp.mean(floats * floats, axis=-1, keepdims=True)
    normed = (floats * lax.rsqrt(meansq + 1e-06) * gain).astype(jnp.bfloat16)
    packed = jnp.dot(normed, weight_in, preferred_element_type=jnp.float32).astype(jnp.bfloat16)
    width = state.shape[-1]
    mixed = attend(packed[..., :width], packed[..., width : 2 * width], packed[..., 2 * width :], line)
    update = jnp.dot(mixed, weight_out, preferred_element_type=jnp.float32)
    return (floats + update).astype(jnp.bfloat16)


def general_body(video, norm_gain, qkv_weight, out_weight):
    state = full_block(video, norm_gain[0], qkv_weight[0], out_weight[0], 0)
    state = lax.all_to_all(state, "aa", split_axis=0, concat_axis=1, tiled=True)
    state = full_block(state, norm_gain[1], qkv_weight[1], out_weight[1], 1)
    state = lax.all_to_all(state, "ba", split_axis=1, concat_axis=2, tiled=True)
    state = full_block(state, norm_gain[2], qkv_weight[2], out_weight[2], 2)
    state = lax.all_to_all(state, "ba", split_axis=2, concat_axis=1, tiled=True)
    return lax.all_to_all(state, "aa", split_axis=1, concat_axis=0, tiled=True)


def block_on(x, gain, w_in, w_out, line_of):
    tokens, d = x.shape
    meansq = jnp.mean(x * x, axis=-1, keepdims=True)
    normed = (x * lax.rsqrt(meansq + 1e-06) * gain).astype(jnp.bfloat16)
    packed = jnp.dot(normed, w_in, preferred_element_type=jnp.float32)

    pair = 2 * HEAD_DIM
    lane = lax.broadcasted_iota(jnp.int32, (GROUP, pair), 1)
    low = lane < HEAD_DIM
    scale = 1.0 / math.sqrt(HEAD_DIM)
    keep_low = jnp.where(low, scale, 0.0)
    keep_high = jnp.where(low, 0.0, scale)
    rows = line_of(lax.broadcasted_iota(jnp.int32, (2 * GROUP, GROUP), 0) % GROUP)
    cols = line_of(lax.broadcasted_iota(jnp.int32, (2 * GROUP, GROUP), 1))
    bias = jnp.where(rows == cols, 0.0, -jnp.inf)
    ones = jnp.ones((GROUP, pair), jnp.bfloat16)

    groups = []
    for g in range(tokens // GROUP):
        at = slice(g * GROUP, (g + 1) * GROUP)
        heads = []
        for p in range(d // pair):
            q = packed[at, p * pair : (p + 1) * pair]
            k = packed[at, d + p * pair : d + (p + 1) * pair].astype(jnp.bfloat16)
            v = packed[at, 2 * d + p * pair : 2 * d + (p + 1) * pair].astype(jnp.bfloat16)
            q2 = jnp.concatenate([q * keep_low, q * keep_high], axis=0).astype(jnp.bfloat16)
            s = lax.dot_general(q2, k, (((1,), (1,)), ((), ())), preferred_element_type=jnp.float32)
            s = s + bias
            e = jnp.exp(s - jnp.max(s, axis=-1, keepdims=True)).astype(jnp.bfloat16)
            o = jnp.dot(e, jnp.concatenate([v, ones], axis=1), preferred_element_type=jnp.float32)
            o = jnp.where(jnp.concatenate([low, low], axis=1), o[:GROUP], o[GROUP:])
            heads.append(o[:, :pair] / o[:, pair:])
        groups.append(jnp.concatenate(heads, axis=1))
    mixed = jnp.concatenate(groups, axis=0).astype(jnp.bfloat16)
    return x + jnp.dot(mixed, w_out, preferred_element_type=jnp.float32)


def load_strided(ref, start, size, stride):
    return jnp.concatenate(
        [ref[p, pl.ds(start, size, stride=stride), :] for p in range(ref.shape[0])], axis=1
    )


def kernel(
    sizes, gain_hbm, x_hbm, wi_hbm, wo_hbm, out_ref,
    gain_ref, x_ref, wi_ref, wo_ref, x32, turned, late, send, recv, y1, y1_late, back,
    x_sem, w_sem, send_sem, recv_sem, back_sem, out_sem, own_sem,
):
    frames, rows, cols, n, cores = sizes
    mine = frames // n
    wide = PIECE // mine
    half = cols // 2
    early = half // wide
    few = PIECE // half
    d = x_ref.shape[-1]
    planes = d // LANES
    aa, ba = lax.axis_index("aa"), lax.axis_index("ba")
    me = aa * cores + ba

    x_copies = [
        pltpu.make_async_copy(x_hbm, x_ref, x_sem.at[0]),
        pltpu.make_async_copy(gain_hbm, gain_ref, x_sem.at[1]),
    ]
    w_copies = []
    for b in range(3):
        w_copies.append(pltpu.make_async_copy(wi_hbm.at[b], wi_ref.at[b], w_sem.at[b, 0]))
        w_copies.append(pltpu.make_async_copy(wo_hbm.at[b], wo_ref.at[b], w_sem.at[b, 1]))
    for copy in x_copies + w_copies[:2]:
        copy.start()

    def where(device):
        return {"aa": device // cores, "ba": device % cores}

    near = n // 2
    side = me // near
    others = [(1 - side) * near + lax.rem(me + o, near) for o in range(near)]
    others += [side * near + lax.rem(me + o, near) for o in range(1, near)]

    barrier = pltpu.get_barrier_semaphore()
    for device in others:
        pl.semaphore_signal(barrier, inc=1, device_id=where(device), device_id_type=MESH)
    for copy in x_copies:
        copy.wait()
    for p in range(planes):
        x32[p] = x_ref[:, p * LANES : (p + 1) * LANES].astype(jnp.float32)
    for copy in w_copies[:2]:
        copy.wait()
    for copy in w_copies[2:]:
        copy.start()
    pl.semaphore_wait(barrier, n - 1)

    spots = [(w, f) for w in range(wide) for f in range(mine)]

    def along_frames(ks):
        x = jnp.concatenate(
            [
                load_strided(x32, f * cols + k * wide + w, n, mine * cols)
                for k in ks
                for w, f in spots
            ],
            axis=0,
        )
        return block_on(x, gain_ref[0:1, :], wi_ref[0], wo_ref[0], lambda i: i // frames)

    def give_chunk(k):
        recv[k, ba, aa] = send[k, me]

        for device in others:
            pltpu.make_async_remote_copy(
                src_ref=send.at[k, device], dst_ref=recv.at[k, ba, aa],
                send_sem=send_sem, recv_sem=recv_sem.at[k],
                device_id=where(device), device_id_type=MESH,
            ).start()

    def first(k, c):
        y = along_frames([k])
        for at, (w, f) in enumerate(spots):
            for p in range(planes):
                turned[p, pl.ds(w * mine + f, n, stride=PIECE), :] = y[
                    at * n : (at + 1) * n, p * LANES : (p + 1) * LANES
                ]
        for p in range(planes):
            send[k, :, :, p * LANES : (p + 1) * LANES] = (
                turned[p].astype(jnp.bfloat16).reshape(n, PIECE, LANES)
            )
        give_chunk(k)
        return c

    lax.fori_loop(0, early, first, 0)

    y = along_frames(range(early, 2 * early))
    for at, (k, w, f) in enumerate((k, w, f) for k in range(early) for w, f in spots):
        row = (f // few) * n * PIECE + (k * wide + w) * few + f % few
        for p in range(planes):
            late[p, pl.ds(row, n, stride=PIECE), :] = y[
                at * n : (at + 1) * n, p * LANES : (p + 1) * LANES
            ]
    for h in range(mine // few):
        for p in range(planes):
            send[early + h, :, :, p * LANES : (p + 1) * LANES] = (
                late[p, h * n * PIECE : (h + 1) * n * PIECE]
                .astype(jnp.bfloat16)
                .reshape(n, PIECE, LANES)
            )
        give_chunk(early + h)

    for copy in w_copies[2:]:
        copy.wait()

    def arrived(k):
        pltpu.make_async_copy(send.at[0, 0 : n - 1], send.at[0, 0 : n - 1], recv_sem.at[k]).wait()

    def along_rows(chunks):
        x = chunks.reshape(-1, d).astype(jnp.float32)
        return block_on(x, gain_ref[1:2, :], wi_ref[1], wo_ref[1], lambda i: i % PIECE)

    for k in range(early):
        arrived(k)
    y = along_rows(recv[0:early])
    for k in range(early):
        for at in range(n):
            place = (at * early + k) * PIECE
            come = (k * n + at) * PIECE
            for p in range(planes):
                y1[p, place : place + PIECE, :] = y[
                    come : come + PIECE, p * LANES : (p + 1) * LANES
                ]

    some = GROUP // (cores * cols)

    def third(h, i):
        f = h * few + i
        parts = []
        for r in range(0, rows, some):
            for b in range(cores):
                at = b * rows + r
                parts.append(load_strided(y1, at * half * mine + f, some * half, mine))
                parts.append(load_strided(y1_late, at * half * few + i, some * half, few))
        x = jnp.concatenate(parts, axis=0)
        y = block_on(x, gain_ref[2:3, :], wi_ref[2], wo_ref[2], lambda t: (t // half) % some)
        for at in range(n):
            low = (at // some) * 2 * some * half + (at % some) * half
            high = low + some * half
            piece = jnp.concatenate([y[low : low + half], y[high : high + half]], axis=0)
            back[f, at] = piece.astype(jnp.bfloat16)
        frame = me * mine + f

        def place(device):
            r, b = device // cores, device % cores
            return ((r // some) * cores + b) * some + r % some

        pltpu.make_async_copy(
            back.at[f, place(me)], out_ref.at[frame], own_sem.at[f]
        ).start()

        for device in others:
            pltpu.make_async_remote_copy(
                src_ref=back.at[f, place(device)], dst_ref=out_ref.at[frame],
                send_sem=back_sem, recv_sem=out_sem,
                device_id=where(device), device_id_type=MESH,
            ).start()

    def rest(h, c):
        arrived(early + h)
        y = along_rows(recv[early + h])
        for p in range(planes):
            y1_late[p] = y[:, p * LANES : (p + 1) * LANES]

        def frame_of(i, c):
            third(h, i)
            return c

        return lax.fori_loop(0, few, frame_of, c)

    lax.fori_loop(0, mine // few, rest, 0)

    for f in range(mine):
        pltpu.make_async_copy(back.at[f, 0], out_ref.at[f], own_sem.at[f]).wait()
    for sem, buffer in ((send_sem, send), (back_sem, back)):
        pltpu.make_async_copy(
            buffer.at[:, 0 : n - 1], buffer.at[:, 0 : n - 1], sem
        ).wait()
    total = (n - 1) * mine
    pltpu.make_async_copy(out_ref.at[0:total], out_ref.at[0:total], out_sem).wait()


def kernel_body(sizes, video, norm_gain, qkv_weight, out_weight):
    frames, rows, cols, n, cores = sizes
    d = video.shape[-1]
    tokens = frames * cols
    planes = d // LANES
    mine = frames // n
    chunks = cols * mine // PIECE
    dma = pltpu.SemaphoreType.DMA
    result = pl.pallas_call(
        functools.partial(kernel, sizes),
        out_shape=jax.ShapeDtypeStruct((frames, cols, d), jnp.bfloat16),
        in_specs=[pl.BlockSpec(memory_space=pltpu.HBM)] * 4,
        out_specs=pl.BlockSpec(memory_space=pl.ANY),
        scratch_shapes=[
            pltpu.VMEM(norm_gain.shape, jnp.float32),
            pltpu.VMEM((tokens, d), jnp.bfloat16),
            pltpu.VMEM(qkv_weight.shape, jnp.bfloat16),
            pltpu.VMEM(out_weight.shape, jnp.bfloat16),
            pltpu.VMEM((planes, tokens, LANES), jnp.float32),
            pltpu.VMEM((planes, n * PIECE, LANES), jnp.float32),
            pltpu.VMEM((planes, tokens // 2, LANES), jnp.float32),
            pltpu.VMEM((chunks, n, PIECE, d), jnp.bfloat16),
            pltpu.VMEM((chunks, cores, n // cores, PIECE, d), jnp.bfloat16),
            pltpu.VMEM((planes, tokens // 2, LANES), jnp.float32),
            pltpu.VMEM((planes, n * PIECE, LANES), jnp.float32),
            pltpu.VMEM((mine, n, cols, d), jnp.bfloat16),
            dma((2,)),
            dma((3, 2)),
            dma,
            dma((chunks,)),
            dma,
            dma,
            dma((mine,)),
        ],
        compiler_params=pltpu.CompilerParams(
            collective_id=0, has_side_effects=True, vmem_limit_bytes=52 * 1024 * 1024
        ),
        cost_estimate=pl.CostEstimate(
            flops=2 * tokens * d * 4 * d * 3, bytes_accessed=8 * tokens * d, transcendentals=0
        ),
    )(norm_gain, video.reshape(tokens, d), qkv_weight, out_weight)
    return result.reshape(video.shape)


def fits(frames, rows, cols, n, cores, d):
    if frames % n or n != rows * cores or n % 2 or d % (2 * HEAD_DIM):
        return False
    mine = frames // n
    if PIECE % mine or cols != PIECE or GROUP % frames or rows * PIECE != GROUP:
        return False
    half = cols // 2
    if half % (PIECE // mine) or mine % (PIECE // half):
        return False
    return GROUP % (cores * cols) == 0 and (n * PIECE) % GROUP == 0


def solution(mesh):
    def body(video, norm_gain, qkv_weight, out_weight):
        frames, here, cols, d = video.shape
        cores = mesh.shape["ba"]
        rows = here * mesh.shape["aa"]
        n = mesh.shape["aa"] * cores
        if here == 1 and fits(frames, rows, cols, n, cores, d):
            sizes = (frames, rows, cols, n, cores)
            return kernel_body(sizes, video, norm_gain, qkv_weight, out_weight)
        return general_body(video, norm_gain, qkv_weight, out_weight)

    return jax.shard_map(
        body,
        mesh=mesh,
        in_specs=(P("groups", "aa", "ba", None), P(), P(), P()),
        out_specs=P("groups", "aa", "ba", None),
        check_vma=False,
    )
```

```python
import functools
import math

import jax
import jax.numpy as jnp
from jax import lax
from jax.experimental import pallas as pl
from jax.experimental.pallas import tpu as pltpu
from jax.sharding import PartitionSpec as P

HEADS = 8
HEAD_DIM = 64
PIECE = 16
GROUP = 128
LANES = 128
MESH = pl.DeviceIdType.MESH


score_forms = ("sbcnd,tbcnd->bcnst", "ascnd,atcnd->acnst", "absnd,abtnd->abnst")
mix_forms = ("bcnst,tbcnd->sbcnd", "acnst,atcnd->ascnd", "abnst,abtnd->absnd")


def attend(queries, key_rows, value_rows, line):
    shape = queries.shape
    split = shape[:3] + (HEADS, HEAD_DIM)
    scores = jnp.einsum(
        score_forms[line],
        queries.reshape(split),
        key_rows.reshape(split),
        preferred_element_type=jnp.float32,
    ) * (1.0 / math.sqrt(HEAD_DIM))
    weights = jax.nn.softmax(scores, axis=-1).astype(jnp.bfloat16)
    mixed = jnp.einsum(
        mix_forms[line], weights, value_rows.reshape(split), preferred_element_type=jnp.float32
    )
    return mixed.astype(jnp.bfloat16).reshape(shape)


def full_block(state, gain, weight_in, weight_out, line):
    floats = state.astype(jnp.float32)
    meansq = jnp.mean(floats * floats, axis=-1, keepdims=True)
    normed = (floats * lax.rsqrt(meansq + 1e-06) * gain).astype(jnp.bfloat16)
    packed = jnp.dot(normed, weight_in, preferred_element_type=jnp.float32).astype(jnp.bfloat16)
    width = state.shape[-1]
    mixed = attend(packed[..., :width], packed[..., width : 2 * width], packed[..., 2 * width :], line)
    update = jnp.dot(mixed, weight_out, preferred_element_type=jnp.float32)
    return (floats + update).astype(jnp.bfloat16)


def general_body(video, norm_gain, qkv_weight, out_weight):
    state = full_block(video, norm_gain[0], qkv_weight[0], out_weight[0], 0)
    state = lax.all_to_all(state, "aa", split_axis=0, concat_axis=1, tiled=True)
    state = full_block(state, norm_gain[1], qkv_weight[1], out_weight[1], 1)
    state = lax.all_to_all(state, "ba", split_axis=1, concat_axis=2, tiled=True)
    state = full_block(state, norm_gain[2], qkv_weight[2], out_weight[2], 2)
    state = lax.all_to_all(state, "ba", split_axis=2, concat_axis=1, tiled=True)
    return lax.all_to_all(state, "aa", split_axis=1, concat_axis=0, tiled=True)


def block_on(x, gain, w_in, w_out, line_of):
    tokens, d = x.shape
    meansq = jnp.mean(x * x, axis=-1, keepdims=True)
    normed = (x * lax.rsqrt(meansq + 1e-06) * gain).astype(jnp.bfloat16)
    packed = jnp.dot(normed, w_in, preferred_element_type=jnp.float32)

    pair = 2 * HEAD_DIM
    lane = lax.broadcasted_iota(jnp.int32, (GROUP, pair), 1)
    low = lane < HEAD_DIM
    scale = 1.0 / math.sqrt(HEAD_DIM)
    keep_low = jnp.where(low, scale, 0.0)
    keep_high = jnp.where(low, 0.0, scale)
    rows = line_of(lax.broadcasted_iota(jnp.int32, (2 * GROUP, GROUP), 0) % GROUP)
    cols = line_of(lax.broadcasted_iota(jnp.int32, (2 * GROUP, GROUP), 1))
    bias = jnp.where(rows == cols, 0.0, -jnp.inf)
    ones = jnp.ones((GROUP, pair), jnp.bfloat16)

    groups = []
    for g in range(tokens // GROUP):
        at = slice(g * GROUP, (g + 1) * GROUP)
        heads = []
        for p in range(d // pair):
            q = packed[at, p * pair : (p + 1) * pair]
            k = packed[at, d + p * pair : d + (p + 1) * pair].astype(jnp.bfloat16)
            v = packed[at, 2 * d + p * pair : 2 * d + (p + 1) * pair].astype(jnp.bfloat16)
            q2 = jnp.concatenate([q * keep_low, q * keep_high], axis=0).astype(jnp.bfloat16)
            s = lax.dot_general(q2, k, (((1,), (1,)), ((), ())), preferred_element_type=jnp.float32)
            s = s + bias
            e = jnp.exp(s - jnp.max(s, axis=-1, keepdims=True)).astype(jnp.bfloat16)
            o = jnp.dot(e, jnp.concatenate([v, ones], axis=1), preferred_element_type=jnp.float32)
            o = jnp.where(jnp.concatenate([low, low], axis=1), o[:GROUP], o[GROUP:])
            heads.append(o[:, :pair] / o[:, pair:])
        groups.append(jnp.concatenate(heads, axis=1))
    mixed = jnp.concatenate(groups, axis=0).astype(jnp.bfloat16)
    return x + jnp.dot(mixed, w_out, preferred_element_type=jnp.float32)


def load_strided(ref, start, size, stride):
    return jnp.concatenate(
        [ref[p, pl.ds(start, size, stride=stride), :] for p in range(ref.shape[0])], axis=1
    )


def kernel(
    sizes, gain_hbm, x_hbm, wi_hbm, wo_hbm, out_ref,
    gain_ref, x_ref, wi_ref, wo_ref, x32, turned, late, send, recv, y1, y1_late, back,
    x_sem, w_sem, send_sem, recv_sem, back_sem, out_sem, own_sem,
):
    frames, rows, cols, n, cores = sizes
    mine = frames // n
    wide = PIECE // mine
    half = cols // 2
    early = half // wide
    few = PIECE // half
    d = x_ref.shape[-1]
    planes = d // LANES
    aa, ba = lax.axis_index("aa"), lax.axis_index("ba")
    me = aa * cores + ba

    x_copies = [
        pltpu.make_async_copy(x_hbm, x_ref, x_sem.at[0]),
        pltpu.make_async_copy(gain_hbm, gain_ref, x_sem.at[1]),
    ]
    w_copies = []
    for b in range(3):
        w_copies.append(pltpu.make_async_copy(wi_hbm.at[b], wi_ref.at[b], w_sem.at[b, 0]))
        w_copies.append(pltpu.make_async_copy(wo_hbm.at[b], wo_ref.at[b], w_sem.at[b, 1]))
    for copy in x_copies + w_copies[:2]:
        copy.start()

    def where(device):
        return {"aa": device // cores, "ba": device % cores}

    near = n // 2
    side = me // near
    others = []
    for o in range(near):
        if o:
            others.append(side * near + lax.rem(me + o, near))
        others.append((1 - side) * near + lax.rem(me + o, near))

    barrier = pltpu.get_barrier_semaphore()
    for device in others:
        pl.semaphore_signal(barrier, inc=1, device_id=where(device), device_id_type=MESH)
    for copy in x_copies:
        copy.wait()
    for p in range(planes):
        x32[p] = x_ref[:, p * LANES : (p + 1) * LANES].astype(jnp.float32)
    for copy in w_copies[:2]:
        copy.wait()
    for copy in w_copies[2:]:
        copy.start()
    pl.semaphore_wait(barrier, n - 1)

    spots = [(w, f) for w in range(wide) for f in range(mine)]

    def along_frames(ks):
        x = jnp.concatenate(
            [
                load_strided(x32, f * cols + k * wide + w, n, mine * cols)
                for k in ks
                for w, f in spots
            ],
            axis=0,
        )
        return block_on(x, gain_ref[0:1, :], wi_ref[0], wo_ref[0], lambda i: i // frames)

    def give_chunk(k):
        recv[k, ba, aa] = send[k, me]

        for device in others:
            pltpu.make_async_remote_copy(
                src_ref=send.at[k, device], dst_ref=recv.at[k, ba, aa],
                send_sem=send_sem, recv_sem=recv_sem.at[k],
                device_id=where(device), device_id_type=MESH,
            ).start()

    def first(k, c):
        y = along_frames([k])
        for at, (w, f) in enumerate(spots):
            for p in range(planes):
                turned[p, pl.ds(w * mine + f, n, stride=PIECE), :] = y[
                    at * n : (at + 1) * n, p * LANES : (p + 1) * LANES
                ]
        for p in range(planes):
            send[k, :, :, p * LANES : (p + 1) * LANES] = (
                turned[p].astype(jnp.bfloat16).reshape(n, PIECE, LANES)
            )
        give_chunk(k)
        return c

    lax.fori_loop(0, early, first, 0)

    y = along_frames(range(early, 2 * early))
    for at, (k, w, f) in enumerate((k, w, f) for k in range(early) for w, f in spots):
        row = (f // few) * n * PIECE + (k * wide + w) * few + f % few
        for p in range(planes):
            late[p, pl.ds(row, n, stride=PIECE), :] = y[
                at * n : (at + 1) * n, p * LANES : (p + 1) * LANES
            ]
    for h in range(mine // few):
        for p in range(planes):
            send[early + h, :, :, p * LANES : (p + 1) * LANES] = (
                late[p, h * n * PIECE : (h + 1) * n * PIECE]
                .astype(jnp.bfloat16)
                .reshape(n, PIECE, LANES)
            )
        give_chunk(early + h)

    for copy in w_copies[2:]:
        copy.wait()

    def arrived(k):
        pltpu.make_async_copy(send.at[0, 0 : n - 1], send.at[0, 0 : n - 1], recv_sem.at[k]).wait()

    def along_rows(chunks):
        x = chunks.reshape(-1, d).astype(jnp.float32)
        return block_on(x, gain_ref[1:2, :], wi_ref[1], wo_ref[1], lambda i: i % PIECE)

    for k in range(early):
        arrived(k)
    y = along_rows(recv[0:early])
    for k in range(early):
        for at in range(n):
            place = (at * early + k) * PIECE
            come = (k * n + at) * PIECE
            for p in range(planes):
                y1[p, place : place + PIECE, :] = y[
                    come : come + PIECE, p * LANES : (p + 1) * LANES
                ]

    some = GROUP // (cores * cols)

    def third(h, i):
        f = h * few + i
        parts = []
        for r in range(0, rows, some):
            for b in range(cores):
                at = b * rows + r
                parts.append(load_strided(y1, at * half * mine + f, some * half, mine))
                parts.append(load_strided(y1_late, at * half * few + i, some * half, few))
        x = jnp.concatenate(parts, axis=0)
        y = block_on(x, gain_ref[2:3, :], wi_ref[2], wo_ref[2], lambda t: (t // half) % some)
        for at in range(n):
            low = (at // some) * 2 * some * half + (at % some) * half
            high = low + some * half
            piece = jnp.concatenate([y[low : low + half], y[high : high + half]], axis=0)
            back[f, at] = piece.astype(jnp.bfloat16)
        frame = me * mine + f

        def place(device):
            r, b = device // cores, device % cores
            return ((r // some) * cores + b) * some + r % some

        pltpu.make_async_copy(
            back.at[f, place(me)], out_ref.at[frame], own_sem.at[f]
        ).start()

        for device in others:
            pltpu.make_async_remote_copy(
                src_ref=back.at[f, place(device)], dst_ref=out_ref.at[frame],
                send_sem=back_sem, recv_sem=out_sem,
                device_id=where(device), device_id_type=MESH,
            ).start()

    def rest(h, c):
        arrived(early + h)
        y = along_rows(recv[early + h])
        for p in range(planes):
            y1_late[p] = y[:, p * LANES : (p + 1) * LANES]

        def frame_of(i, c):
            third(h, i)
            return c

        return lax.fori_loop(0, few, frame_of, c)

    lax.fori_loop(0, mine // few, rest, 0)

    for f in range(mine):
        pltpu.make_async_copy(back.at[f, 0], out_ref.at[f], own_sem.at[f]).wait()
    for sem, buffer in ((send_sem, send), (back_sem, back)):
        pltpu.make_async_copy(
            buffer.at[:, 0 : n - 1], buffer.at[:, 0 : n - 1], sem
        ).wait()
    total = (n - 1) * mine
    pltpu.make_async_copy(out_ref.at[0:total], out_ref.at[0:total], out_sem).wait()


def kernel_body(sizes, video, norm_gain, qkv_weight, out_weight):
    frames, rows, cols, n, cores = sizes
    d = video.shape[-1]
    tokens = frames * cols
    planes = d // LANES
    mine = frames // n
    chunks = cols * mine // PIECE
    dma = pltpu.SemaphoreType.DMA
    result = pl.pallas_call(
        functools.partial(kernel, sizes),
        out_shape=jax.ShapeDtypeStruct((frames, cols, d), jnp.bfloat16),
        in_specs=[pl.BlockSpec(memory_space=pltpu.HBM)] * 4,
        out_specs=pl.BlockSpec(memory_space=pl.ANY),
        scratch_shapes=[
            pltpu.VMEM(norm_gain.shape, jnp.float32),
            pltpu.VMEM((tokens, d), jnp.bfloat16),
            pltpu.VMEM(qkv_weight.shape, jnp.bfloat16),
            pltpu.VMEM(out_weight.shape, jnp.bfloat16),
            pltpu.VMEM((planes, tokens, LANES), jnp.float32),
            pltpu.VMEM((planes, n * PIECE, LANES), jnp.float32),
            pltpu.VMEM((planes, tokens // 2, LANES), jnp.float32),
            pltpu.VMEM((chunks, n, PIECE, d), jnp.bfloat16),
            pltpu.VMEM((chunks, cores, n // cores, PIECE, d), jnp.bfloat16),
            pltpu.VMEM((planes, tokens // 2, LANES), jnp.float32),
            pltpu.VMEM((planes, n * PIECE, LANES), jnp.float32),
            pltpu.VMEM((mine, n, cols, d), jnp.bfloat16),
            dma((2,)),
            dma((3, 2)),
            dma,
            dma((chunks,)),
            dma,
            dma,
            dma((mine,)),
        ],
        compiler_params=pltpu.CompilerParams(
            collective_id=0, has_side_effects=True, vmem_limit_bytes=52 * 1024 * 1024
        ),
        cost_estimate=pl.CostEstimate(
            flops=2 * tokens * d * 4 * d * 3, bytes_accessed=8 * tokens * d, transcendentals=0
        ),
    )(norm_gain, video.reshape(tokens, d), qkv_weight, out_weight)
    return result.reshape(video.shape)


def fits(frames, rows, cols, n, cores, d):
    if frames % n or n != rows * cores or n % 2 or d % (2 * HEAD_DIM):
        return False
    mine = frames // n
    if PIECE % mine or cols != PIECE or GROUP % frames or rows * PIECE != GROUP:
        return False
    half = cols // 2
    if half % (PIECE // mine) or mine % (PIECE // half):
        return False
    return GROUP % (cores * cols) == 0 and (n * PIECE) % GROUP == 0


def solution(mesh):
    def body(video, norm_gain, qkv_weight, out_weight):
        frames, here, cols, d = video.shape
        cores = mesh.shape["ba"]
        rows = here * mesh.shape["aa"]
        n = mesh.shape["aa"] * cores
        if here == 1 and fits(frames, rows, cols, n, cores, d):
            sizes = (frames, rows, cols, n, cores)
            return kernel_body(sizes, video, norm_gain, qkv_weight, out_weight)
        return general_body(video, norm_gain, qkv_weight, out_weight)

    return jax.shard_map(
        body,
        mesh=mesh,
        in_specs=(P("groups", "aa", "ba", None), P(), P(), P()),
        out_specs=P("groups", "aa", "ba", None),
        check_vma=False,
    )
```

```python
import functools
import math

import jax
import jax.numpy as jnp
from jax import lax
from jax.experimental import pallas as pl
from jax.experimental.pallas import tpu as pltpu
from jax.sharding import PartitionSpec as P

HEADS = 8
HEAD_DIM = 64
PIECE = 16
GROUP = 128
LANES = 128
MESH = pl.DeviceIdType.MESH


score_forms = ("sbcnd,tbcnd->bcnst", "ascnd,atcnd->acnst", "absnd,abtnd->abnst")
mix_forms = ("bcnst,tbcnd->sbcnd", "acnst,atcnd->ascnd", "abnst,abtnd->absnd")


def attend(queries, key_rows, value_rows, line):
    shape = queries.shape
    split = shape[:3] + (HEADS, HEAD_DIM)
    scores = jnp.einsum(
        score_forms[line],
        queries.reshape(split),
        key_rows.reshape(split),
        preferred_element_type=jnp.float32,
    ) * (1.0 / math.sqrt(HEAD_DIM))
    weights = jax.nn.softmax(scores, axis=-1).astype(jnp.bfloat16)
    mixed = jnp.einsum(
        mix_forms[line], weights, value_rows.reshape(split), preferred_element_type=jnp.float32
    )
    return mixed.astype(jnp.bfloat16).reshape(shape)


def full_block(state, gain, weight_in, weight_out, line):
    floats = state.astype(jnp.float32)
    meansq = jnp.mean(floats * floats, axis=-1, keepdims=True)
    normed = (floats * lax.rsqrt(meansq + 1e-06) * gain).astype(jnp.bfloat16)
    packed = jnp.dot(normed, weight_in, preferred_element_type=jnp.float32).astype(jnp.bfloat16)
    width = state.shape[-1]
    mixed = attend(packed[..., :width], packed[..., width : 2 * width], packed[..., 2 * width :], line)
    update = jnp.dot(mixed, weight_out, preferred_element_type=jnp.float32)
    return (floats + update).astype(jnp.bfloat16)


def general_body(video, norm_gain, qkv_weight, out_weight):
    state = full_block(video, norm_gain[0], qkv_weight[0], out_weight[0], 0)
    state = lax.all_to_all(state, "aa", split_axis=0, concat_axis=1, tiled=True)
    state = full_block(state, norm_gain[1], qkv_weight[1], out_weight[1], 1)
    state = lax.all_to_all(state, "ba", split_axis=1, concat_axis=2, tiled=True)
    state = full_block(state, norm_gain[2], qkv_weight[2], out_weight[2], 2)
    state = lax.all_to_all(state, "ba", split_axis=2, concat_axis=1, tiled=True)
    return lax.all_to_all(state, "aa", split_axis=1, concat_axis=0, tiled=True)


def mask_of(line_of):
    rows = line_of(lax.broadcasted_iota(jnp.int32, (2 * GROUP, GROUP), 0) % GROUP)
    cols = line_of(lax.broadcasted_iota(jnp.int32, (2 * GROUP, GROUP), 1))
    return jnp.where(rows == cols, 0.0, -jnp.inf)


def block_on(x, gain, w_in, w_out, bias_ref):
    tokens, d = x.shape
    meansq = jnp.mean(x * x, axis=-1, keepdims=True)
    normed = (x * lax.rsqrt(meansq + 1e-06) * gain).astype(jnp.bfloat16)
    packed = jnp.dot(normed, w_in, preferred_element_type=jnp.float32).astype(jnp.bfloat16)

    pair = 2 * HEAD_DIM
    lane = lax.broadcasted_iota(jnp.int32, (GROUP, pair), 1)
    low = lane < HEAD_DIM
    scale = 1.0 / math.sqrt(HEAD_DIM)
    keep_low = jnp.where(low, scale, 0.0).astype(jnp.bfloat16)
    keep_high = jnp.where(low, 0.0, scale).astype(jnp.bfloat16)
    ones = jnp.ones((GROUP, pair), jnp.bfloat16)

    groups = []
    for g in range(tokens // GROUP):
        at = slice(g * GROUP, (g + 1) * GROUP)
        heads = []
        for p in range(d // pair):
            q = packed[at, p * pair : (p + 1) * pair]
            k = packed[at, d + p * pair : d + (p + 1) * pair]
            v = packed[at, 2 * d + p * pair : 2 * d + (p + 1) * pair]
            q2 = jnp.concatenate([q * keep_low, q * keep_high], axis=0)
            s = lax.dot_general(q2, k, (((1,), (1,)), ((), ())), preferred_element_type=jnp.float32)
            s = s + bias_ref[...]
            e = jnp.exp(s - jnp.max(s, axis=-1, keepdims=True)).astype(jnp.bfloat16)
            o = jnp.dot(e, jnp.concatenate([v, ones], axis=1), preferred_element_type=jnp.float32)
            o = jnp.where(jnp.concatenate([low, low], axis=1), o[:GROUP], o[GROUP:])
            total = o[:, pair:]
            inverse = pl.reciprocal(total, approx=True)
            inverse = inverse * (2.0 - total * inverse)
            heads.append(o[:, :pair] * inverse)
        groups.append(jnp.concatenate(heads, axis=1))
    mixed = jnp.concatenate(groups, axis=0).astype(jnp.bfloat16)
    return x + jnp.dot(mixed, w_out, preferred_element_type=jnp.float32)


def load_strided(ref, start, size, stride):
    return jnp.concatenate(
        [ref[p, pl.ds(start, size, stride=stride), :] for p in range(ref.shape[0])], axis=1
    )


def kernel(
    sizes, gain_hbm, x_hbm, wi_hbm, wo_hbm, out_ref,
    bias_ref, gain_ref, x_ref, wi_ref, wo_ref, x32, turned, late, send, recv, y1, y1_late, back,
    x_sem, w_sem, send_sem, recv_sem, back_sem, out_sem, own_sem,
):
    frames, rows, cols, n, cores = sizes
    mine = frames // n
    wide = PIECE // mine
    half = cols // 2
    early = half // wide
    few = PIECE // half
    some = GROUP // (cores * cols)
    d = x_ref.shape[-1]
    planes = d // LANES
    aa, ba = lax.axis_index("aa"), lax.axis_index("ba")
    me = aa * cores + ba

    x_copies = [
        pltpu.make_async_copy(x_hbm, x_ref, x_sem.at[0]),
        pltpu.make_async_copy(gain_hbm, gain_ref, x_sem.at[1]),
    ]
    w_copies = []
    for b in range(3):
        w_copies.append(pltpu.make_async_copy(wi_hbm.at[b], wi_ref.at[b], w_sem.at[b, 0]))
        w_copies.append(pltpu.make_async_copy(wo_hbm.at[b], wo_ref.at[b], w_sem.at[b, 1]))
    for copy in x_copies + w_copies[:2]:
        copy.start()

    def where(device):
        return {"aa": device // cores, "ba": device % cores}

    near = n // 2
    side = me // near
    others = [(1 - side) * near + lax.rem(me + o, near) for o in range(near)]
    others += [side * near + lax.rem(me + o, near) for o in range(1, near)]

    barrier = pltpu.get_barrier_semaphore()
    for device in others:
        pl.semaphore_signal(barrier, inc=1, device_id=where(device), device_id_type=MESH)
    bias_ref[0] = mask_of(lambda i: i // frames)
    bias_ref[1] = mask_of(lambda i: i % PIECE)
    bias_ref[2] = mask_of(lambda i: (i // half) % some)
    for copy in x_copies:
        copy.wait()
    for p in range(planes):
        x32[p] = x_ref[:, p * LANES : (p + 1) * LANES].astype(jnp.float32)
    for copy in w_copies[:2]:
        copy.wait()
    for copy in w_copies[2:]:
        copy.start()
    pl.semaphore_wait(barrier, n - 1)

    spots = [(w, f) for w in range(wide) for f in range(mine)]

    def along_frames(ks):
        x = jnp.concatenate(
            [
                load_strided(x32, f * cols + k * wide + w, n, mine * cols)
                for k in ks
                for w, f in spots
            ],
            axis=0,
        )
        return block_on(x, gain_ref[0:1, :], wi_ref[0], wo_ref[0], bias_ref.at[0])

    def give_chunk(k):
        recv[k, ba, aa] = send[k, me]

        for device in others:
            pltpu.make_async_remote_copy(
                src_ref=send.at[k, device], dst_ref=recv.at[k, ba, aa],
                send_sem=send_sem, recv_sem=recv_sem.at[k],
                device_id=where(device), device_id_type=MESH,
            ).start()

    def first(k, c):
        y = along_frames([k])
        for at, (w, f) in enumerate(spots):
            for p in range(planes):
                turned[p, pl.ds(w * mine + f, n, stride=PIECE), :] = y[
                    at * n : (at + 1) * n, p * LANES : (p + 1) * LANES
                ]
        for p in range(planes):
            send[k, :, :, p * LANES : (p + 1) * LANES] = (
                turned[p].astype(jnp.bfloat16).reshape(n, PIECE, LANES)
            )
        give_chunk(k)
        return c

    lax.fori_loop(0, early, first, 0)

    y = along_frames(range(early, 2 * early))
    for at, (k, w, f) in enumerate((k, w, f) for k in range(early) for w, f in spots):
        row = (f // few) * n * PIECE + (k * wide + w) * few + f % few
        for p in range(planes):
            late[p, pl.ds(row, n, stride=PIECE), :] = y[
                at * n : (at + 1) * n, p * LANES : (p + 1) * LANES
            ]
    for h in range(mine // few):
        for p in range(planes):
            send[early + h, :, :, p * LANES : (p + 1) * LANES] = (
                late[p, h * n * PIECE : (h + 1) * n * PIECE]
                .astype(jnp.bfloat16)
                .reshape(n, PIECE, LANES)
            )
        give_chunk(early + h)

    for copy in w_copies[2:]:
        copy.wait()

    def arrived(k):
        pltpu.make_async_copy(send.at[0, 0 : n - 1], send.at[0, 0 : n - 1], recv_sem.at[k]).wait()

    def along_rows(chunks):
        x = chunks.reshape(-1, d).astype(jnp.float32)
        return block_on(x, gain_ref[1:2, :], wi_ref[1], wo_ref[1], bias_ref.at[1])

    for k in range(early):
        arrived(k)
    y = along_rows(recv[0:early])
    for k in range(early):
        for at in range(n):
            place = (at * early + k) * PIECE
            come = (k * n + at) * PIECE
            for p in range(planes):
                y1[p, place : place + PIECE, :] = y[
                    come : come + PIECE, p * LANES : (p + 1) * LANES
                ]


    def third(h, i):
        f = h * few + i
        parts = []
        for r in range(0, rows, some):
            for b in range(cores):
                at = b * rows + r
                parts.append(load_strided(y1, at * half * mine + f, some * half, mine))
                parts.append(load_strided(y1_late, at * half * few + i, some * half, few))
        x = jnp.concatenate(parts, axis=0)
        y = block_on(x, gain_ref[2:3, :], wi_ref[2], wo_ref[2], bias_ref.at[2])
        for at in range(n):
            low = (at // some) * 2 * some * half + (at % some) * half
            high = low + some * half
            piece = jnp.concatenate([y[low : low + half], y[high : high + half]], axis=0)
            back[f, at] = piece.astype(jnp.bfloat16)
        frame = me * mine + f

        def place(device):
            r, b = device // cores, device % cores
            return ((r // some) * cores + b) * some + r % some

        pltpu.make_async_copy(
            back.at[f, place(me)], out_ref.at[frame], own_sem.at[f]
        ).start()

        for device in others:
            pltpu.make_async_remote_copy(
                src_ref=back.at[f, place(device)], dst_ref=out_ref.at[frame],
                send_sem=back_sem, recv_sem=out_sem,
                device_id=where(device), device_id_type=MESH,
            ).start()

    def rest(h, c):
        arrived(early + h)
        y = along_rows(recv[early + h])
        for p in range(planes):
            y1_late[p] = y[:, p * LANES : (p + 1) * LANES]

        def frame_of(i, c):
            third(h, i)
            return c

        return lax.fori_loop(0, few, frame_of, c)

    lax.fori_loop(0, mine // few, rest, 0)

    for f in range(mine):
        pltpu.make_async_copy(back.at[f, 0], out_ref.at[f], own_sem.at[f]).wait()
    for sem, buffer in ((send_sem, send), (back_sem, back)):
        pltpu.make_async_copy(
            buffer.at[:, 0 : n - 1], buffer.at[:, 0 : n - 1], sem
        ).wait()
    total = (n - 1) * mine
    pltpu.make_async_copy(out_ref.at[0:total], out_ref.at[0:total], out_sem).wait()


def kernel_body(sizes, video, norm_gain, qkv_weight, out_weight):
    frames, rows, cols, n, cores = sizes
    d = video.shape[-1]
    tokens = frames * cols
    planes = d // LANES
    mine = frames // n
    chunks = cols * mine // PIECE
    dma = pltpu.SemaphoreType.DMA
    result = pl.pallas_call(
        functools.partial(kernel, sizes),
        out_shape=jax.ShapeDtypeStruct((frames, cols, d), jnp.bfloat16),
        in_specs=[pl.BlockSpec(memory_space=pltpu.HBM)] * 4,
        out_specs=pl.BlockSpec(memory_space=pl.ANY),
        scratch_shapes=[
            pltpu.VMEM((3, 2 * GROUP, GROUP), jnp.float32),
            pltpu.VMEM(norm_gain.shape, jnp.float32),
            pltpu.VMEM((tokens, d), jnp.bfloat16),
            pltpu.VMEM(qkv_weight.shape, jnp.bfloat16),
            pltpu.VMEM(out_weight.shape, jnp.bfloat16),
            pltpu.VMEM((planes, tokens, LANES), jnp.float32),
            pltpu.VMEM((planes, n * PIECE, LANES), jnp.float32),
            pltpu.VMEM((planes, tokens // 2, LANES), jnp.float32),
            pltpu.VMEM((chunks, n, PIECE, d), jnp.bfloat16),
            pltpu.VMEM((chunks, cores, n // cores, PIECE, d), jnp.bfloat16),
            pltpu.VMEM((planes, tokens // 2, LANES), jnp.float32),
            pltpu.VMEM((planes, n * PIECE, LANES), jnp.float32),
            pltpu.VMEM((mine, n, cols, d), jnp.bfloat16),
            dma((2,)),
            dma((3, 2)),
            dma,
            dma((chunks,)),
            dma,
            dma,
            dma((mine,)),
        ],
        compiler_params=pltpu.CompilerParams(
            collective_id=0, has_side_effects=True, vmem_limit_bytes=52 * 1024 * 1024
        ),
        cost_estimate=pl.CostEstimate(
            flops=2 * tokens * d * 4 * d * 3, bytes_accessed=8 * tokens * d, transcendentals=0
        ),
    )(norm_gain, video.reshape(tokens, d), qkv_weight, out_weight)
    return result.reshape(video.shape)


def fits(frames, rows, cols, n, cores, d):
    if frames % n or n != rows * cores or n % 2 or d % (2 * HEAD_DIM):
        return False
    mine = frames // n
    if PIECE % mine or cols != PIECE or GROUP % frames or rows * PIECE != GROUP:
        return False
    half = cols // 2
    if half % (PIECE // mine) or mine % (PIECE // half):
        return False
    return GROUP % (cores * cols) == 0 and (n * PIECE) % GROUP == 0


def solution(mesh):
    def body(video, norm_gain, qkv_weight, out_weight):
        frames, here, cols, d = video.shape
        cores = mesh.shape["ba"]
        rows = here * mesh.shape["aa"]
        n = mesh.shape["aa"] * cores
        if here == 1 and fits(frames, rows, cols, n, cores, d):
            sizes = (frames, rows, cols, n, cores)
            return kernel_body(sizes, video, norm_gain, qkv_weight, out_weight)
        return general_body(video, norm_gain, qkv_weight, out_weight)

    return jax.shard_map(
        body,
        mesh=mesh,
        in_specs=(P("groups", "aa", "ba", None), P(), P(), P()),
        out_specs=P("groups", "aa", "ba", None),
        check_vma=False,
    )
```

```python
import functools
import math

import jax
import jax.numpy as jnp
from jax import lax
from jax.experimental import pallas as pl
from jax.experimental.pallas import tpu as pltpu
from jax.sharding import PartitionSpec as P

HEADS = 8
HEAD_DIM = 64
PIECE = 16
GROUP = 128
LANES = 128
MESH = pl.DeviceIdType.MESH


score_forms = ("sbcnd,tbcnd->bcnst", "ascnd,atcnd->acnst", "absnd,abtnd->abnst")
mix_forms = ("bcnst,tbcnd->sbcnd", "acnst,atcnd->ascnd", "abnst,abtnd->absnd")


def attend(queries, key_rows, value_rows, line):
    shape = queries.shape
    split = shape[:3] + (HEADS, HEAD_DIM)
    scores = jnp.einsum(
        score_forms[line],
        queries.reshape(split),
        key_rows.reshape(split),
        preferred_element_type=jnp.float32,
    ) * (1.0 / math.sqrt(HEAD_DIM))
    weights = jax.nn.softmax(scores, axis=-1).astype(jnp.bfloat16)
    mixed = jnp.einsum(
        mix_forms[line], weights, value_rows.reshape(split), preferred_element_type=jnp.float32
    )
    return mixed.astype(jnp.bfloat16).reshape(shape)


def full_block(state, gain, weight_in, weight_out, line):
    floats = state.astype(jnp.float32)
    meansq = jnp.mean(floats * floats, axis=-1, keepdims=True)
    normed = (floats * lax.rsqrt(meansq + 1e-06) * gain).astype(jnp.bfloat16)
    packed = jnp.dot(normed, weight_in, preferred_element_type=jnp.float32).astype(jnp.bfloat16)
    width = state.shape[-1]
    mixed = attend(packed[..., :width], packed[..., width : 2 * width], packed[..., 2 * width :], line)
    update = jnp.dot(mixed, weight_out, preferred_element_type=jnp.float32)
    return (floats + update).astype(jnp.bfloat16)


def general_body(video, norm_gain, qkv_weight, out_weight):
    state = full_block(video, norm_gain[0], qkv_weight[0], out_weight[0], 0)
    state = lax.all_to_all(state, "aa", split_axis=0, concat_axis=1, tiled=True)
    state = full_block(state, norm_gain[1], qkv_weight[1], out_weight[1], 1)
    state = lax.all_to_all(state, "ba", split_axis=1, concat_axis=2, tiled=True)
    state = full_block(state, norm_gain[2], qkv_weight[2], out_weight[2], 2)
    state = lax.all_to_all(state, "ba", split_axis=2, concat_axis=1, tiled=True)
    return lax.all_to_all(state, "aa", split_axis=1, concat_axis=0, tiled=True)


def mask_of(line_of):
    rows = line_of(lax.broadcasted_iota(jnp.int32, (2 * GROUP, GROUP), 0) % GROUP)
    cols = line_of(lax.broadcasted_iota(jnp.int32, (2 * GROUP, GROUP), 1))
    return jnp.where(rows == cols, 0.0, -jnp.inf)


def block_on(x, gain, w_in_ref, w_out_ref, masks, before_out=None):
    tokens, d = x.shape
    meansq = jnp.mean(x * x, axis=-1, keepdims=True)
    normed = (x * lax.rsqrt(meansq + 1e-06) * gain).astype(jnp.bfloat16)
    packed = jnp.dot(normed, w_in_ref[...], preferred_element_type=jnp.float32).astype(jnp.bfloat16)

    pair = 2 * HEAD_DIM
    lane = lax.broadcasted_iota(jnp.int32, (GROUP, pair), 1)
    low = lane < HEAD_DIM
    scale = 1.0 / math.sqrt(HEAD_DIM)
    keep_low = jnp.where(low, scale, 0.0).astype(jnp.bfloat16)
    keep_high = jnp.where(low, 0.0, scale).astype(jnp.bfloat16)
    ones = jnp.ones((GROUP, pair), jnp.bfloat16)

    groups = []
    for g in range(tokens // GROUP):
        at = slice(g * GROUP, (g + 1) * GROUP)
        heads = []
        for p in range(d // pair):
            q = packed[at, p * pair : (p + 1) * pair]
            k = packed[at, d + p * pair : d + (p + 1) * pair]
            v = packed[at, 2 * d + p * pair : 2 * d + (p + 1) * pair]
            q2 = jnp.concatenate([q * keep_low, q * keep_high], axis=0)
            s = lax.dot_general(q2, k, (((1,), (1,)), ((), ())), preferred_element_type=jnp.float32)
            s = s + masks[g][...]
            e = jnp.exp(s - jnp.max(s, axis=-1, keepdims=True)).astype(jnp.bfloat16)
            o = jnp.dot(e, jnp.concatenate([v, ones], axis=1), preferred_element_type=jnp.float32)
            o = jnp.where(jnp.concatenate([low, low], axis=1), o[:GROUP], o[GROUP:])
            total = o[:, pair:]
            inverse = pl.reciprocal(total, approx=True)
            inverse = inverse * (2.0 - total * inverse)
            heads.append(o[:, :pair] * inverse)
        groups.append(jnp.concatenate(heads, axis=1))
    mixed = jnp.concatenate(groups, axis=0).astype(jnp.bfloat16)
    if before_out is not None:
        before_out()
    return x + jnp.dot(mixed, w_out_ref[...], preferred_element_type=jnp.float32)


def load_strided(ref, start, size, stride):
    return jnp.concatenate(
        [ref[p, pl.ds(start, size, stride=stride), :] for p in range(ref.shape[0])], axis=1
    )


def kernel(
    sizes, gain_hbm, x_hbm, wi_hbm, wo_hbm, out_ref,
    bias_ref, gain_ref, x_ref, wi_ref, wo_ref, x32, turned, late, send_short, recv_short, send, recv, y1, y1_late, back,
    x_sem, w_sem, short_sem, send_sem, recv_sem, back_sem, out_sem, own_sem,
):
    frames, rows, cols, n, cores = sizes
    mine = frames // n
    wide = PIECE // mine
    half = cols // 2
    early = half // wide
    few = PIECE // half
    some = GROUP // (cores * cols)
    d = x_ref.shape[-1]
    planes = d // LANES
    short = PIECE // 2
    aa, ba = lax.axis_index("aa"), lax.axis_index("ba")
    me = aa * cores + ba

    x_copies = [
        pltpu.make_async_copy(x_hbm, x_ref, x_sem.at[0]),
        pltpu.make_async_copy(gain_hbm, gain_ref, x_sem.at[1]),
    ]
    w_copies = []
    for b in range(3):
        w_copies.append(pltpu.make_async_copy(wi_hbm.at[b], wi_ref.at[b], w_sem.at[b, 0]))
        w_copies.append(pltpu.make_async_copy(wo_hbm.at[b], wo_ref.at[b], w_sem.at[b, 1]))
    for copy in x_copies + w_copies[:2]:
        copy.start()

    def where(device):
        return {"aa": device // cores, "ba": device % cores}

    near = n // 2
    side = me // near
    others = [(1 - side) * near + lax.rem(me + o, near) for o in range(near)]
    others += [side * near + lax.rem(me + o, near) for o in range(1, near)]

    barrier = pltpu.get_barrier_semaphore()
    for device in others:
        pl.semaphore_signal(barrier, inc=1, device_id=where(device), device_id_type=MESH)
    bias_ref[0] = mask_of(lambda i: i // frames)
    bias_ref[1] = mask_of(lambda i: i % PIECE)
    bias_ref[2] = mask_of(lambda i: (i // half) % some)
    bias_ref[3] = mask_of(lambda i: i // (rows * short) * short + i % short)
    for copy in x_copies:
        copy.wait()
    for p in range(planes):
        x32[p] = x_ref[:, p * LANES : (p + 1) * LANES].astype(jnp.float32)
    w_copies[0].wait()

    spots = [(w, f) for w in range(wide) for f in range(mine)]

    def along_frames(ks, spots, before_out=None):
        x = jnp.concatenate(
            [
                load_strided(x32, f * cols + k * wide + w, n, mine * cols)
                for k in ks
                for w, f in spots
            ],
            axis=0,
        )
        masks = [bias_ref.at[0]] * (x.shape[0] // GROUP)
        return block_on(x, gain_ref[0:1, :], wi_ref.at[0], wo_ref.at[0], masks, before_out)

    def give_chunk(k):
        recv[k, ba, aa] = send[k, me]

        for device in others:
            pltpu.make_async_remote_copy(
                src_ref=send.at[k, device], dst_ref=recv.at[k, ba, aa],
                send_sem=send_sem, recv_sem=recv_sem.at[k],
                device_id=where(device), device_id_type=MESH,
            ).start()

    def more_weights():
        w_copies[1].wait()
        for copy in w_copies[2:]:
            copy.start()

    for part in range(2):
        these = spots[part * short : (part + 1) * short]
        y = along_frames([0], these, None if part else more_weights)
        for at in range(short):
            for p in range(planes):
                row = p // (planes // 2) * short + at
                turned[p % (planes // 2), pl.ds(row, n, stride=PIECE), :] = y[
                    at * n : (at + 1) * n, p * LANES : (p + 1) * LANES
                ]
        for p in range(planes // 2):
            send_short[part, :, :, p * LANES : (p + 1) * LANES] = (
                turned[p].astype(jnp.bfloat16).reshape(n, PIECE, LANES)
            )
        recv_short[part, ba, aa] = send_short[part, me]
        if part == 0:
            pl.semaphore_wait(barrier, n - 1)
        for device in others:
            pltpu.make_async_remote_copy(
                src_ref=send_short.at[part, device], dst_ref=recv_short.at[part, ba, aa],
                send_sem=short_sem.at[2], recv_sem=short_sem.at[part],
                device_id=where(device), device_id_type=MESH,
            ).start()

    for k in range(1, early):
        y = along_frames([k], spots)
        for at, (w, f) in enumerate(spots):
            for p in range(planes):
                turned[p, pl.ds(w * mine + f, n, stride=PIECE), :] = y[
                    at * n : (at + 1) * n, p * LANES : (p + 1) * LANES
                ]
        for p in range(planes):
            send[k, :, :, p * LANES : (p + 1) * LANES] = (
                turned[p].astype(jnp.bfloat16).reshape(n, PIECE, LANES)
            )
        give_chunk(k)

    y = along_frames(range(early, 2 * early), spots)
    for at, (k, w, f) in enumerate((k, w, f) for k in range(early) for w, f in spots):
        row = (f // few) * n * PIECE + (k * wide + w) * few + f % few
        for p in range(planes):
            late[p, pl.ds(row, n, stride=PIECE), :] = y[
                at * n : (at + 1) * n, p * LANES : (p + 1) * LANES
            ]
    for h in range(mine // few):
        for p in range(planes):
            send[early + h, :, :, p * LANES : (p + 1) * LANES] = (
                late[p, h * n * PIECE : (h + 1) * n * PIECE]
                .astype(jnp.bfloat16)
                .reshape(n, PIECE, LANES)
            )
        give_chunk(early + h)

    for copy in w_copies[2:]:
        copy.wait()

    def arrived(k):
        pltpu.make_async_copy(send.at[0, 0 : n - 1], send.at[0, 0 : n - 1], recv_sem.at[k]).wait()

    def along_rows(x, masks):
        return block_on(x, gain_ref[1:2, :], wi_ref.at[1], wo_ref.at[1], masks)

    parts = []
    for part in range(2):
        all_short = send_short.at[0, 0 : n - 1]
        pltpu.make_async_copy(all_short, all_short, short_sem.at[part]).wait()
        x = recv_short[part].reshape(n, PIECE, d // 2).astype(jnp.float32)
        x = jnp.concatenate([x[:, :short], x[:, short:]], axis=-1)
        parts.append(x.reshape(n * short, d))
    for k in range(1, early):
        arrived(k)
        parts.append(recv[k].reshape(n * PIECE, d).astype(jnp.float32))
    x = jnp.concatenate(parts, axis=0)
    y = along_rows(x, [bias_ref.at[3]] * 2 + [bias_ref.at[1]] * (x.shape[0] // GROUP - 2))
    moves = [
        (at * early * PIECE + part * short, (part * n + at) * short, short)
        for part in range(2)
        for at in range(n)
    ]
    moves += [
        ((at * early + k) * PIECE, (k * n + at) * PIECE, PIECE)
        for k in range(1, early)
        for at in range(n)
    ]
    for place, come, size in moves:
        for p in range(planes):
            y1[p, place : place + size, :] = y[come : come + size, p * LANES : (p + 1) * LANES]


    def third(h, i):
        f = h * few + i
        parts = []
        for r in range(0, rows, some):
            for b in range(cores):
                at = b * rows + r
                parts.append(load_strided(y1, at * half * mine + f, some * half, mine))
                parts.append(load_strided(y1_late, at * half * few + i, some * half, few))
        x = jnp.concatenate(parts, axis=0)
        masks = [bias_ref.at[2]] * (rows // some)
        y = block_on(x, gain_ref[2:3, :], wi_ref.at[2], wo_ref.at[2], masks)
        for at in range(n):
            low = (at // some) * 2 * some * half + (at % some) * half
            high = low + some * half
            piece = jnp.concatenate([y[low : low + half], y[high : high + half]], axis=0)
            back[f, at] = piece.astype(jnp.bfloat16)
        frame = me * mine + f

        def place(device):
            r, b = device // cores, device % cores
            return ((r // some) * cores + b) * some + r % some

        pltpu.make_async_copy(
            back.at[f, place(me)], out_ref.at[frame], own_sem.at[f]
        ).start()

        for device in others:
            pltpu.make_async_remote_copy(
                src_ref=back.at[f, place(device)], dst_ref=out_ref.at[frame],
                send_sem=back_sem, recv_sem=out_sem,
                device_id=where(device), device_id_type=MESH,
            ).start()

    def rest(h, c):
        arrived(early + h)
        x = recv[early + h].reshape(n * PIECE, d).astype(jnp.float32)
        y = along_rows(x, [bias_ref.at[1]] * (x.shape[0] // GROUP))
        for p in range(planes):
            y1_late[p] = y[:, p * LANES : (p + 1) * LANES]

        def frame_of(i, c):
            third(h, i)
            return c

        return lax.fori_loop(0, few, frame_of, c)

    lax.fori_loop(0, mine // few, rest, 0)

    for f in range(mine):
        pltpu.make_async_copy(back.at[f, 0], out_ref.at[f], own_sem.at[f]).wait()
    for sem, buffer in ((short_sem.at[2], send_short), (send_sem, send.at[1:]), (back_sem, back)):
        pltpu.make_async_copy(
            buffer.at[:, 0 : n - 1], buffer.at[:, 0 : n - 1], sem
        ).wait()
    total = (n - 1) * mine
    pltpu.make_async_copy(out_ref.at[0:total], out_ref.at[0:total], out_sem).wait()


def kernel_body(sizes, video, norm_gain, qkv_weight, out_weight):
    frames, rows, cols, n, cores = sizes
    d = video.shape[-1]
    tokens = frames * cols
    planes = d // LANES
    mine = frames // n
    chunks = cols * mine // PIECE
    dma = pltpu.SemaphoreType.DMA
    result = pl.pallas_call(
        functools.partial(kernel, sizes),
        out_shape=jax.ShapeDtypeStruct((frames, cols, d), jnp.bfloat16),
        in_specs=[pl.BlockSpec(memory_space=pltpu.HBM)] * 4,
        out_specs=pl.BlockSpec(memory_space=pl.ANY),
        scratch_shapes=[
            pltpu.VMEM((4, 2 * GROUP, GROUP), jnp.float32),
            pltpu.VMEM(norm_gain.shape, jnp.float32),
            pltpu.VMEM((tokens, d), jnp.bfloat16),
            pltpu.VMEM(qkv_weight.shape, jnp.bfloat16),
            pltpu.VMEM(out_weight.shape, jnp.bfloat16),
            pltpu.VMEM((planes, tokens, LANES), jnp.float32),
            pltpu.VMEM((planes, n * PIECE, LANES), jnp.float32),
            pltpu.VMEM((planes, tokens // 2, LANES), jnp.float32),
            pltpu.VMEM((2, n, PIECE, d // 2), jnp.bfloat16),
            pltpu.VMEM((2, cores, n // cores, PIECE, d // 2), jnp.bfloat16),
            pltpu.VMEM((chunks, n, PIECE, d), jnp.bfloat16),
            pltpu.VMEM((chunks, cores, n // cores, PIECE, d), jnp.bfloat16),
            pltpu.VMEM((planes, tokens // 2, LANES), jnp.float32),
            pltpu.VMEM((planes, n * PIECE, LANES), jnp.float32),
            pltpu.VMEM((mine, n, cols, d), jnp.bfloat16),
            dma((2,)),
            dma((3, 2)),
            dma((3,)),
            dma,
            dma((chunks,)),
            dma,
            dma,
            dma((mine,)),
        ],
        compiler_params=pltpu.CompilerParams(
            collective_id=0, has_side_effects=True, vmem_limit_bytes=52 * 1024 * 1024
        ),
        cost_estimate=pl.CostEstimate(
            flops=2 * tokens * d * 4 * d * 3, bytes_accessed=8 * tokens * d, transcendentals=0
        ),
    )(norm_gain, video.reshape(tokens, d), qkv_weight, out_weight)
    return result.reshape(video.shape)


def fits(frames, rows, cols, n, cores, d):
    if frames % n or n != rows * cores or n % 2 or d % (2 * HEAD_DIM):
        return False
    mine = frames // n
    if PIECE % mine or cols != PIECE or GROUP % frames or rows * PIECE != GROUP:
        return False
    half = cols // 2
    if half % (PIECE // mine) or mine % (PIECE // half):
        return False
    if PIECE // mine % 2 or n * PIECE != 2 * GROUP or d % (2 * LANES):
        return False
    return GROUP % (cores * cols) == 0 and (n * PIECE) % GROUP == 0


def solution(mesh):
    def body(video, norm_gain, qkv_weight, out_weight):
        frames, here, cols, d = video.shape
        cores = mesh.shape["ba"]
        rows = here * mesh.shape["aa"]
        n = mesh.shape["aa"] * cores
        if here == 1 and fits(frames, rows, cols, n, cores, d):
            sizes = (frames, rows, cols, n, cores)
            return kernel_body(sizes, video, norm_gain, qkv_weight, out_weight)
        return general_body(video, norm_gain, qkv_weight, out_weight)

    return jax.shard_map(
        body,
        mesh=mesh,
        in_specs=(P("groups", "aa", "ba", None), P(), P(), P()),
        out_specs=P("groups", "aa", "ba", None),
        check_vma=False,
    )
```

```python
import functools
import math

import jax
import jax.numpy as jnp
from jax import lax
from jax.experimental import pallas as pl
from jax.experimental.pallas import tpu as pltpu
from jax.sharding import PartitionSpec as P

HEADS = 8
HEAD_DIM = 64
PIECE = 16
GROUP = 128
LANES = 128
MESH = pl.DeviceIdType.MESH


score_forms = ("sbcnd,tbcnd->bcnst", "ascnd,atcnd->acnst", "absnd,abtnd->abnst")
mix_forms = ("bcnst,tbcnd->sbcnd", "acnst,atcnd->ascnd", "abnst,abtnd->absnd")


def attend(queries, key_rows, value_rows, line):
    shape = queries.shape
    split = shape[:3] + (HEADS, HEAD_DIM)
    scores = jnp.einsum(
        score_forms[line],
        queries.reshape(split),
        key_rows.reshape(split),
        preferred_element_type=jnp.float32,
    ) * (1.0 / math.sqrt(HEAD_DIM))
    weights = jax.nn.softmax(scores, axis=-1).astype(jnp.bfloat16)
    mixed = jnp.einsum(
        mix_forms[line], weights, value_rows.reshape(split), preferred_element_type=jnp.float32
    )
    return mixed.astype(jnp.bfloat16).reshape(shape)


def full_block(state, gain, weight_in, weight_out, line):
    floats = state.astype(jnp.float32)
    meansq = jnp.mean(floats * floats, axis=-1, keepdims=True)
    normed = (floats * lax.rsqrt(meansq + 1e-06) * gain).astype(jnp.bfloat16)
    packed = jnp.dot(normed, weight_in, preferred_element_type=jnp.float32).astype(jnp.bfloat16)
    width = state.shape[-1]
    mixed = attend(packed[..., :width], packed[..., width : 2 * width], packed[..., 2 * width :], line)
    update = jnp.dot(mixed, weight_out, preferred_element_type=jnp.float32)
    return (floats + update).astype(jnp.bfloat16)


def general_body(video, norm_gain, qkv_weight, out_weight):
    state = full_block(video, norm_gain[0], qkv_weight[0], out_weight[0], 0)
    state = lax.all_to_all(state, "aa", split_axis=0, concat_axis=1, tiled=True)
    state = full_block(state, norm_gain[1], qkv_weight[1], out_weight[1], 1)
    state = lax.all_to_all(state, "ba", split_axis=1, concat_axis=2, tiled=True)
    state = full_block(state, norm_gain[2], qkv_weight[2], out_weight[2], 2)
    state = lax.all_to_all(state, "ba", split_axis=2, concat_axis=1, tiled=True)
    return lax.all_to_all(state, "aa", split_axis=1, concat_axis=0, tiled=True)


def mask_of(line_of):
    rows = line_of(lax.broadcasted_iota(jnp.int32, (2 * GROUP, GROUP), 0) % GROUP)
    cols = line_of(lax.broadcasted_iota(jnp.int32, (2 * GROUP, GROUP), 1))
    return jnp.where(rows == cols, 0.0, -jnp.inf)


def block_on(x, gain, w_in_ref, w_out_ref, masks, before_out=None):
    tokens, d = x.shape
    meansq = jnp.mean(x * x, axis=-1, keepdims=True)
    normed = (x * lax.rsqrt(meansq + 1e-06) * gain).astype(jnp.bfloat16)
    packed = jnp.dot(normed, w_in_ref[...], preferred_element_type=jnp.float32).astype(jnp.bfloat16)

    pair = 2 * HEAD_DIM
    lane = lax.broadcasted_iota(jnp.int32, (GROUP, pair), 1)
    low = lane < HEAD_DIM
    scale = 1.0 / math.sqrt(HEAD_DIM)
    keep_low = jnp.where(low, scale, 0.0).astype(jnp.bfloat16)
    keep_high = jnp.where(low, 0.0, scale).astype(jnp.bfloat16)
    ones = jnp.ones((GROUP, pair), jnp.bfloat16)

    groups = []
    for g in range(tokens // GROUP):
        at = slice(g * GROUP, (g + 1) * GROUP)
        heads = []
        for p in range(d // pair):
            q = packed[at, p * pair : (p + 1) * pair]
            k = packed[at, d + p * pair : d + (p + 1) * pair]
            v = packed[at, 2 * d + p * pair : 2 * d + (p + 1) * pair]
            q2 = jnp.concatenate([q * keep_low, q * keep_high], axis=0)
            s = lax.dot_general(q2, k, (((1,), (1,)), ((), ())), preferred_element_type=jnp.float32)
            s = s + masks[g][...]
            e = jnp.exp(s - jnp.max(s, axis=-1, keepdims=True)).astype(jnp.bfloat16)
            o = jnp.dot(e, jnp.concatenate([v, ones], axis=1), preferred_element_type=jnp.float32)
            o = jnp.where(jnp.concatenate([low, low], axis=1), o[:GROUP], o[GROUP:])
            total = o[:, pair:]
            inverse = pl.reciprocal(total, approx=True)
            inverse = inverse * (2.0 - total * inverse)
            heads.append(o[:, :pair] * inverse)
        groups.append(jnp.concatenate(heads, axis=1))
    mixed = jnp.concatenate(groups, axis=0).astype(jnp.bfloat16)
    if before_out is not None:
        before_out()
    return x + jnp.dot(mixed, w_out_ref[...], preferred_element_type=jnp.float32)


def load_strided(ref, start, size, stride):
    return jnp.concatenate(
        [ref[p, pl.ds(start, size, stride=stride), :] for p in range(ref.shape[0])], axis=1
    )


def kernel(
    sizes, gain_hbm, x_hbm, wi_hbm, wo_hbm, out_ref,
    bias_ref, gain_ref, x_ref, wi_ref, wo_ref, x32, turned, late, send_short, recv_short, send, recv, y1, y1_late, back,
    x_sem, w_sem, short_sem, send_sem, recv_sem, back_sem, out_sem, own_sem,
):
    frames, rows, cols, n, cores = sizes
    mine = frames // n
    wide = PIECE // mine
    half = cols // 2
    early = half // wide
    few = PIECE // half
    some = GROUP // (cores * cols)
    d = x_ref.shape[-1]
    planes = d // LANES
    short = PIECE // 2
    aa, ba = lax.axis_index("aa"), lax.axis_index("ba")
    me = aa * cores + ba

    x_copies = [
        pltpu.make_async_copy(x_hbm, x_ref, x_sem.at[0]),
        pltpu.make_async_copy(gain_hbm, gain_ref, x_sem.at[1]),
    ]
    w_copies = []
    for b in range(3):
        w_copies.append(pltpu.make_async_copy(wi_hbm.at[b], wi_ref.at[b], w_sem.at[b, 0]))
        w_copies.append(pltpu.make_async_copy(wo_hbm.at[b], wo_ref.at[b], w_sem.at[b, 1]))
    for copy in x_copies + w_copies[:2]:
        copy.start()

    def where(device):
        return {"aa": device // cores, "ba": device % cores}

    near = n // 2
    side = me // near
    others = [(1 - side) * near + lax.rem(me + o, near) for o in range(near)]
    others += [side * near + lax.rem(me + o, near) for o in range(1, near)]

    barrier = pltpu.get_barrier_semaphore()
    for device in others:
        pl.semaphore_signal(barrier, inc=1, device_id=where(device), device_id_type=MESH)
    bias_ref[0] = mask_of(lambda i: i // frames)
    bias_ref[1] = mask_of(lambda i: i % PIECE)
    bias_ref[2] = mask_of(lambda i: (i // half) % some)
    bias_ref[3] = mask_of(lambda i: i // (rows * short) * short + i % short)
    for copy in x_copies:
        copy.wait()
    for p in range(planes):
        x32[p] = x_ref[:, p * LANES : (p + 1) * LANES].astype(jnp.float32)
    w_copies[0].wait()

    spots = [(w, f) for w in range(wide) for f in range(mine)]

    def along_frames(ks, spots, before_out=None):
        x = jnp.concatenate(
            [
                load_strided(x32, f * cols + k * wide + w, n, mine * cols)
                for k in ks
                for w, f in spots
            ],
            axis=0,
        )
        masks = [bias_ref.at[0]] * (x.shape[0] // GROUP)
        return block_on(x, gain_ref[0:1, :], wi_ref.at[0], wo_ref.at[0], masks, before_out)

    def give_chunk(k):
        recv[k, ba, aa] = send[k, me]

        for device in others:
            pltpu.make_async_remote_copy(
                src_ref=send.at[k, device], dst_ref=recv.at[k, ba, aa],
                send_sem=send_sem, recv_sem=recv_sem.at[k],
                device_id=where(device), device_id_type=MESH,
            ).start()

    def more_weights():
        w_copies[1].wait()
        for copy in w_copies[2:]:
            copy.start()

    for part in range(2):
        these = spots[part * short : (part + 1) * short]
        y = along_frames([0], these, None if part else more_weights)
        for at in range(short):
            for p in range(planes):
                row = p // (planes // 2) * short + at
                turned[p % (planes // 2), pl.ds(row, n, stride=PIECE), :] = y[
                    at * n : (at + 1) * n, p * LANES : (p + 1) * LANES
                ]
        for p in range(planes // 2):
            send_short[part, :, :, p * LANES : (p + 1) * LANES] = (
                turned[p].astype(jnp.bfloat16).reshape(n, PIECE, LANES)
            )
        recv_short[part, ba, aa] = send_short[part, me]
        if part == 0:
            pl.semaphore_wait(barrier, n - 1)
        for device in others:
            pltpu.make_async_remote_copy(
                src_ref=send_short.at[part, device], dst_ref=recv_short.at[part, ba, aa],
                send_sem=short_sem.at[2], recv_sem=short_sem.at[part],
                device_id=where(device), device_id_type=MESH,
            ).start()

    for k in range(1, early):
        y = along_frames([k], spots)
        for at, (w, f) in enumerate(spots):
            for p in range(planes):
                turned[p, pl.ds(w * mine + f, n, stride=PIECE), :] = y[
                    at * n : (at + 1) * n, p * LANES : (p + 1) * LANES
                ]
        for p in range(planes):
            send[k, :, :, p * LANES : (p + 1) * LANES] = (
                turned[p].astype(jnp.bfloat16).reshape(n, PIECE, LANES)
            )
        give_chunk(k)

    y = along_frames(range(early, 2 * early), spots)
    for at, (k, w, f) in enumerate((k, w, f) for k in range(early) for w, f in spots):
        row = (f // few) * n * PIECE + (k * wide + w) * few + f % few
        for p in range(planes):
            late[p, pl.ds(row, n, stride=PIECE), :] = y[
                at * n : (at + 1) * n, p * LANES : (p + 1) * LANES
            ]
    for h in range(mine // few):
        for p in range(planes):
            send[early + h, :, :, p * LANES : (p + 1) * LANES] = (
                late[p, h * n * PIECE : (h + 1) * n * PIECE]
                .astype(jnp.bfloat16)
                .reshape(n, PIECE, LANES)
            )
        give_chunk(early + h)

    for copy in w_copies[2:]:
        copy.wait()

    def arrived(k):
        pltpu.make_async_copy(send.at[0, 0 : n - 1], send.at[0, 0 : n - 1], recv_sem.at[k]).wait()

    def along_rows(x, masks):
        return block_on(x, gain_ref[1:2, :], wi_ref.at[1], wo_ref.at[1], masks)

    parts = []
    for part in range(2):
        all_short = send_short.at[0, 0 : n - 1]
        pltpu.make_async_copy(all_short, all_short, short_sem.at[part]).wait()
        x = recv_short[part].reshape(n, PIECE, d // 2).astype(jnp.float32)
        x = jnp.concatenate([x[:, :short], x[:, short:]], axis=-1)
        parts.append(x.reshape(n * short, d))
    for k in range(1, early):
        arrived(k)
        parts.append(recv[k].reshape(n * PIECE, d).astype(jnp.float32))
    x = jnp.concatenate(parts, axis=0)
    y = along_rows(x, [bias_ref.at[3]] * 2 + [bias_ref.at[1]] * (x.shape[0] // GROUP - 2))
    moves = [
        (at * early * PIECE + part * short, (part * n + at) * short, short)
        for part in range(2)
        for at in range(n)
    ]
    moves += [
        ((at * early + k) * PIECE, (k * n + at) * PIECE, PIECE)
        for k in range(1, early)
        for at in range(n)
    ]
    for place, come, size in moves:
        for p in range(planes):
            y1[p, place : place + size, :] = y[come : come + size, p * LANES : (p + 1) * LANES]


    def third(h, i):
        f = h * few + i
        frame = me * mine + f
        for g, part in enumerate((1 - side, side)):
            parts = []
            for b in range(cores):
                at = b * rows + part * some
                parts.append(load_strided(y1, at * half * mine + f, some * half, mine))
                parts.append(load_strided(y1_late, at * half * few + i, some * half, few))
            x = jnp.concatenate(parts, axis=0)
            y = block_on(x, gain_ref[2:3, :], wi_ref.at[2], wo_ref.at[2], [bias_ref.at[2]])
            for b in range(cores):
                for r in range(some):
                    low = (b * 2 * some + r) * half
                    high = low + some * half
                    piece = jnp.concatenate([y[low : low + half], y[high : high + half]], axis=0)
                    back[f, g * near + r * cores + b] = piece.astype(jnp.bfloat16)
            if g:
                pltpu.make_async_copy(
                    back.at[f, near + lax.rem(me, near)], out_ref.at[frame], own_sem.at[f]
                ).start()
            for o in range(g, near):
                turn = lax.rem(me + o, near)
                pltpu.make_async_remote_copy(
                    src_ref=back.at[f, g * near + turn], dst_ref=out_ref.at[frame],
                    send_sem=back_sem, recv_sem=out_sem,
                    device_id=where(part * near + turn), device_id_type=MESH,
                ).start()

    def rest(h, c):
        arrived(early + h)
        x = recv[early + h].reshape(n * PIECE, d).astype(jnp.float32)
        y = along_rows(x, [bias_ref.at[1]] * (x.shape[0] // GROUP))
        for p in range(planes):
            y1_late[p] = y[:, p * LANES : (p + 1) * LANES]

        def frame_of(i, c):
            third(h, i)
            return c

        return lax.fori_loop(0, few, frame_of, c)

    lax.fori_loop(0, mine // few, rest, 0)

    for f in range(mine):
        pltpu.make_async_copy(back.at[f, 0], out_ref.at[f], own_sem.at[f]).wait()
    for sem, buffer in ((short_sem.at[2], send_short), (send_sem, send.at[1:]), (back_sem, back)):
        pltpu.make_async_copy(
            buffer.at[:, 0 : n - 1], buffer.at[:, 0 : n - 1], sem
        ).wait()
    total = (n - 1) * mine
    pltpu.make_async_copy(out_ref.at[0:total], out_ref.at[0:total], out_sem).wait()


def kernel_body(sizes, video, norm_gain, qkv_weight, out_weight):
    frames, rows, cols, n, cores = sizes
    d = video.shape[-1]
    tokens = frames * cols
    planes = d // LANES
    mine = frames // n
    chunks = cols * mine // PIECE
    dma = pltpu.SemaphoreType.DMA
    result = pl.pallas_call(
        functools.partial(kernel, sizes),
        out_shape=jax.ShapeDtypeStruct((frames, cols, d), jnp.bfloat16),
        in_specs=[pl.BlockSpec(memory_space=pltpu.HBM)] * 4,
        out_specs=pl.BlockSpec(memory_space=pl.ANY),
        scratch_shapes=[
            pltpu.VMEM((4, 2 * GROUP, GROUP), jnp.float32),
            pltpu.VMEM(norm_gain.shape, jnp.float32),
            pltpu.VMEM((tokens, d), jnp.bfloat16),
            pltpu.VMEM(qkv_weight.shape, jnp.bfloat16),
            pltpu.VMEM(out_weight.shape, jnp.bfloat16),
            pltpu.VMEM((planes, tokens, LANES), jnp.float32),
            pltpu.VMEM((planes, n * PIECE, LANES), jnp.float32),
            pltpu.VMEM((planes, tokens // 2, LANES), jnp.float32),
            pltpu.VMEM((2, n, PIECE, d // 2), jnp.bfloat16),
            pltpu.VMEM((2, cores, n // cores, PIECE, d // 2), jnp.bfloat16),
            pltpu.VMEM((chunks, n, PIECE, d), jnp.bfloat16),
            pltpu.VMEM((chunks, cores, n // cores, PIECE, d), jnp.bfloat16),
            pltpu.VMEM((planes, tokens // 2, LANES), jnp.float32),
            pltpu.VMEM((planes, n * PIECE, LANES), jnp.float32),
            pltpu.VMEM((mine, n, cols, d), jnp.bfloat16),
            dma((2,)),
            dma((3, 2)),
            dma((3,)),
            dma,
            dma((chunks,)),
            dma,
            dma,
            dma((mine,)),
        ],
        compiler_params=pltpu.CompilerParams(
            collective_id=0, has_side_effects=True, vmem_limit_bytes=52 * 1024 * 1024
        ),
        cost_estimate=pl.CostEstimate(
            flops=2 * tokens * d * 4 * d * 3, bytes_accessed=8 * tokens * d, transcendentals=0
        ),
    )(norm_gain, video.reshape(tokens, d), qkv_weight, out_weight)
    return result.reshape(video.shape)


def fits(frames, rows, cols, n, cores, d):
    if frames % n or n != rows * cores or n % 2 or d % (2 * HEAD_DIM):
        return False
    mine = frames // n
    if PIECE % mine or cols != PIECE or GROUP % frames or rows * PIECE != GROUP:
        return False
    half = cols // 2
    if half % (PIECE // mine) or mine % (PIECE // half):
        return False
    if PIECE // mine % 2 or n * PIECE != 2 * GROUP or rows * cores * cols != 2 * GROUP or d % (2 * LANES):
        return False
    return GROUP % (cores * cols) == 0 and (n * PIECE) % GROUP == 0


def solution(mesh):
    def body(video, norm_gain, qkv_weight, out_weight):
        frames, here, cols, d = video.shape
        cores = mesh.shape["ba"]
        rows = here * mesh.shape["aa"]
        n = mesh.shape["aa"] * cores
        if here == 1 and fits(frames, rows, cols, n, cores, d):
            sizes = (frames, rows, cols, n, cores)
            return kernel_body(sizes, video, norm_gain, qkv_weight, out_weight)
        return general_body(video, norm_gain, qkv_weight, out_weight)

    return jax.shard_map(
        body,
        mesh=mesh,
        in_specs=(P("groups", "aa", "ba", None), P(), P(), P()),
        out_specs=P("groups", "aa", "ba", None),
        check_vma=False,
    )
```

```python
import functools
import math

import jax
import jax.numpy as jnp
from jax import lax
from jax.experimental import pallas as pl
from jax.experimental.pallas import tpu as pltpu
from jax.sharding import PartitionSpec as P

HEADS = 8
HEAD_DIM = 64
PIECE = 16
GROUP = 128
LANES = 128
MESH = pl.DeviceIdType.MESH


score_forms = ("sbcnd,tbcnd->bcnst", "ascnd,atcnd->acnst", "absnd,abtnd->abnst")
mix_forms = ("bcnst,tbcnd->sbcnd", "acnst,atcnd->ascnd", "abnst,abtnd->absnd")


def attend(queries, key_rows, value_rows, line):
    shape = queries.shape
    split = shape[:3] + (HEADS, HEAD_DIM)
    scores = jnp.einsum(
        score_forms[line],
        queries.reshape(split),
        key_rows.reshape(split),
        preferred_element_type=jnp.float32,
    ) * (1.0 / math.sqrt(HEAD_DIM))
    weights = jax.nn.softmax(scores, axis=-1).astype(jnp.bfloat16)
    mixed = jnp.einsum(
        mix_forms[line], weights, value_rows.reshape(split), preferred_element_type=jnp.float32
    )
    return mixed.astype(jnp.bfloat16).reshape(shape)


def full_block(state, gain, weight_in, weight_out, line):
    floats = state.astype(jnp.float32)
    meansq = jnp.mean(floats * floats, axis=-1, keepdims=True)
    normed = (floats * lax.rsqrt(meansq + 1e-06) * gain).astype(jnp.bfloat16)
    packed = jnp.dot(normed, weight_in, preferred_element_type=jnp.float32).astype(jnp.bfloat16)
    width = state.shape[-1]
    mixed = attend(packed[..., :width], packed[..., width : 2 * width], packed[..., 2 * width :], line)
    update = jnp.dot(mixed, weight_out, preferred_element_type=jnp.float32)
    return (floats + update).astype(jnp.bfloat16)


def general_body(video, norm_gain, qkv_weight, out_weight):
    state = full_block(video, norm_gain[0], qkv_weight[0], out_weight[0], 0)
    state = lax.all_to_all(state, "aa", split_axis=0, concat_axis=1, tiled=True)
    state = full_block(state, norm_gain[1], qkv_weight[1], out_weight[1], 1)
    state = lax.all_to_all(state, "ba", split_axis=1, concat_axis=2, tiled=True)
    state = full_block(state, norm_gain[2], qkv_weight[2], out_weight[2], 2)
    state = lax.all_to_all(state, "ba", split_axis=2, concat_axis=1, tiled=True)
    return lax.all_to_all(state, "aa", split_axis=1, concat_axis=0, tiled=True)


def mask_of(line_of):
    rows = line_of(lax.broadcasted_iota(jnp.int32, (2 * GROUP, GROUP), 0) % GROUP)
    cols = line_of(lax.broadcasted_iota(jnp.int32, (2 * GROUP, GROUP), 1))
    return jnp.where(rows == cols, 0.0, -jnp.inf)


def block_on(x, gain, w_in_ref, w_out_ref, masks, before_out=None):
    tokens, d = x.shape
    meansq = jnp.mean(x * x, axis=-1, keepdims=True)
    normed = (x * lax.rsqrt(meansq + 1e-06) * gain).astype(jnp.bfloat16)
    packed = jnp.dot(normed, w_in_ref[...], preferred_element_type=jnp.float32).astype(jnp.bfloat16)

    pair = 2 * HEAD_DIM
    lane = lax.broadcasted_iota(jnp.int32, (GROUP, pair), 1)
    low = lane < HEAD_DIM
    scale = 1.0 / math.sqrt(HEAD_DIM)
    keep_low = jnp.where(low, scale, 0.0).astype(jnp.bfloat16)
    keep_high = jnp.where(low, 0.0, scale).astype(jnp.bfloat16)
    ones = jnp.ones((GROUP, pair), jnp.bfloat16)

    groups = []
    for g in range(tokens // GROUP):
        at = slice(g * GROUP, (g + 1) * GROUP)
        heads = []
        for p in range(d // pair):
            q = packed[at, p * pair : (p + 1) * pair]
            k = packed[at, d + p * pair : d + (p + 1) * pair]
            v = packed[at, 2 * d + p * pair : 2 * d + (p + 1) * pair]
            q2 = jnp.concatenate([q * keep_low, q * keep_high], axis=0)
            s = lax.dot_general(q2, k, (((1,), (1,)), ((), ())), preferred_element_type=jnp.float32)
            s = s + masks[g][...]
            e = jnp.exp(s - jnp.max(s, axis=-1, keepdims=True)).astype(jnp.bfloat16)
            o = jnp.dot(e, jnp.concatenate([v, ones], axis=1), preferred_element_type=jnp.float32)
            o = jnp.where(jnp.concatenate([low, low], axis=1), o[:GROUP], o[GROUP:])
            total = o[:, pair:]
            inverse = pl.reciprocal(total, approx=True)
            inverse = inverse * (2.0 - total * inverse)
            heads.append(o[:, :pair] * inverse)
        groups.append(jnp.concatenate(heads, axis=1))
    mixed = jnp.concatenate(groups, axis=0).astype(jnp.bfloat16)
    if before_out is not None:
        before_out()
    return x + jnp.dot(mixed, w_out_ref[...], preferred_element_type=jnp.float32)


def load_strided(ref, start, size, stride):
    return jnp.concatenate(
        [ref[p, pl.ds(start, size, stride=stride), :] for p in range(ref.shape[0])], axis=1
    )


def kernel(
    sizes, gain_hbm, x_hbm, wi_hbm, wo_hbm, out_ref,
    bias_ref, gain_ref, x_ref, wi_ref, wo_ref, x32, turned, late, send_short, recv_short, send, recv, y1, y1_late, back,
    x_sem, w_sem, short_sem, send_sem, recv_sem, back_sem, out_sem, own_sem,
):
    frames, rows, cols, n, cores = sizes
    mine = frames // n
    wide = PIECE // mine
    half = cols // 2
    early = half // wide
    few = PIECE // half
    some = GROUP // (cores * cols)
    d = x_ref.shape[-1]
    planes = d // LANES
    short = PIECE // 2
    aa, ba = lax.axis_index("aa"), lax.axis_index("ba")
    me = aa * cores + ba

    x_copies = [
        pltpu.make_async_copy(x_hbm, x_ref, x_sem.at[0]),
        pltpu.make_async_copy(gain_hbm, gain_ref, x_sem.at[1]),
    ]
    w_copies = []
    for b in range(3):
        w_copies.append(pltpu.make_async_copy(wi_hbm.at[b], wi_ref.at[b], w_sem.at[b, 0]))
        w_copies.append(pltpu.make_async_copy(wo_hbm.at[b], wo_ref.at[b], w_sem.at[b, 1]))
    for copy in x_copies + w_copies[:2]:
        copy.start()

    def where(device):
        return {"aa": device // cores, "ba": device % cores}

    near = n // 2
    side = me // near
    others = [(1 - side) * near + lax.rem(me + o, near) for o in range(near)]
    others += [side * near + lax.rem(me + o, near) for o in range(1, near)]

    barrier = pltpu.get_barrier_semaphore()
    for device in others:
        pl.semaphore_signal(barrier, inc=1, device_id=where(device), device_id_type=MESH)
    bias_ref[0] = mask_of(lambda i: i // frames)
    for copy in x_copies:
        copy.wait()
    for p in range(planes):
        x32[p] = x_ref[:, p * LANES : (p + 1) * LANES].astype(jnp.float32)
    w_copies[0].wait()

    spots = [(w, f) for w in range(wide) for f in range(mine)]

    def along_frames(ks, spots, before_out=None):
        x = jnp.concatenate(
            [
                load_strided(x32, f * cols + k * wide + w, n, mine * cols)
                for k in ks
                for w, f in spots
            ],
            axis=0,
        )
        masks = [bias_ref.at[0]] * (x.shape[0] // GROUP)
        return block_on(x, gain_ref[0:1, :], wi_ref.at[0], wo_ref.at[0], masks, before_out)

    def give_chunk(k):
        recv[k, ba, aa] = send[k, me]

        for device in others:
            pltpu.make_async_remote_copy(
                src_ref=send.at[k, device], dst_ref=recv.at[k, ba, aa],
                send_sem=send_sem, recv_sem=recv_sem.at[k],
                device_id=where(device), device_id_type=MESH,
            ).start()

    def more_weights():
        w_copies[1].wait()
        for copy in w_copies[2:]:
            copy.start()

    for part in range(2):
        these = spots[part * short : (part + 1) * short]
        y = along_frames([0], these, None if part else more_weights)
        for at in range(short):
            for p in range(planes):
                row = p // (planes // 2) * short + at
                turned[p % (planes // 2), pl.ds(row, n, stride=PIECE), :] = y[
                    at * n : (at + 1) * n, p * LANES : (p + 1) * LANES
                ]
        for p in range(planes // 2):
            send_short[part, :, :, p * LANES : (p + 1) * LANES] = (
                turned[p].astype(jnp.bfloat16).reshape(n, PIECE, LANES)
            )
        recv_short[part, ba, aa] = send_short[part, me]
        if part == 0:
            pl.semaphore_wait(barrier, n - 1)
        for device in others:
            pltpu.make_async_remote_copy(
                src_ref=send_short.at[part, device], dst_ref=recv_short.at[part, ba, aa],
                send_sem=short_sem.at[2], recv_sem=short_sem.at[part],
                device_id=where(device), device_id_type=MESH,
            ).start()

    bias_ref[1] = mask_of(lambda i: i % PIECE)
    bias_ref[2] = mask_of(lambda i: (i // half) % some)
    bias_ref[3] = mask_of(lambda i: i // (rows * short) * short + i % short)

    for k in range(1, early):
        y = along_frames([k], spots)
        for at, (w, f) in enumerate(spots):
            for p in range(planes):
                turned[p, pl.ds(w * mine + f, n, stride=PIECE), :] = y[
                    at * n : (at + 1) * n, p * LANES : (p + 1) * LANES
                ]
        for p in range(planes):
            send[k, :, :, p * LANES : (p + 1) * LANES] = (
                turned[p].astype(jnp.bfloat16).reshape(n, PIECE, LANES)
            )
        give_chunk(k)

    y = along_frames(range(early, 2 * early), spots)
    for at, (k, w, f) in enumerate((k, w, f) for k in range(early) for w, f in spots):
        row = (f // few) * n * PIECE + (k * wide + w) * few + f % few
        for p in range(planes):
            late[p, pl.ds(row, n, stride=PIECE), :] = y[
                at * n : (at + 1) * n, p * LANES : (p + 1) * LANES
            ]
    for h in range(mine // few):
        for p in range(planes):
            send[early + h, :, :, p * LANES : (p + 1) * LANES] = (
                late[p, h * n * PIECE : (h + 1) * n * PIECE]
                .astype(jnp.bfloat16)
                .reshape(n, PIECE, LANES)
            )
        give_chunk(early + h)

    for copy in w_copies[2:]:
        copy.wait()

    def arrived(k):
        pltpu.make_async_copy(send.at[0, 0 : n - 1], send.at[0, 0 : n - 1], recv_sem.at[k]).wait()

    def along_rows(x, masks):
        return block_on(x, gain_ref[1:2, :], wi_ref.at[1], wo_ref.at[1], masks)

    parts = []
    for part in range(2):
        all_short = send_short.at[0, 0 : n - 1]
        pltpu.make_async_copy(all_short, all_short, short_sem.at[part]).wait()
        x = recv_short[part].reshape(n, PIECE, d // 2).astype(jnp.float32)
        x = jnp.concatenate([x[:, :short], x[:, short:]], axis=-1)
        parts.append(x.reshape(n * short, d))
    for k in range(1, early):
        arrived(k)
        parts.append(recv[k].reshape(n * PIECE, d).astype(jnp.float32))
    x = jnp.concatenate(parts, axis=0)
    y = along_rows(x, [bias_ref.at[3]] * 2 + [bias_ref.at[1]] * (x.shape[0] // GROUP - 2))
    moves = [
        (at * early * PIECE + part * short, (part * n + at) * short, short)
        for part in range(2)
        for at in range(n)
    ]
    moves += [
        ((at * early + k) * PIECE, (k * n + at) * PIECE, PIECE)
        for k in range(1, early)
        for at in range(n)
    ]
    for place, come, size in moves:
        for p in range(planes):
            y1[p, place : place + size, :] = y[come : come + size, p * LANES : (p + 1) * LANES]


    def third(h, i):
        f = h * few + i
        frame = me * mine + f
        for g, part in enumerate((1 - side, side)):
            parts = []
            for b in range(cores):
                at = b * rows + part * some
                parts.append(load_strided(y1, at * half * mine + f, some * half, mine))
                parts.append(load_strided(y1_late, at * half * few + i, some * half, few))
            x = jnp.concatenate(parts, axis=0)
            y = block_on(x, gain_ref[2:3, :], wi_ref.at[2], wo_ref.at[2], [bias_ref.at[2]])
            for b in range(cores):
                for r in range(some):
                    low = (b * 2 * some + r) * half
                    high = low + some * half
                    piece = jnp.concatenate([y[low : low + half], y[high : high + half]], axis=0)
                    back[f, g * near + r * cores + b] = piece.astype(jnp.bfloat16)
            if g:
                pltpu.make_async_copy(
                    back.at[f, near + lax.rem(me, near)], out_ref.at[frame], own_sem.at[f]
                ).start()
            for o in range(g, near):
                turn = lax.rem(me + o, near)
                pltpu.make_async_remote_copy(
                    src_ref=back.at[f, g * near + turn], dst_ref=out_ref.at[frame],
                    send_sem=back_sem, recv_sem=out_sem,
                    device_id=where(part * near + turn), device_id_type=MESH,
                ).start()

    def rest(h, c):
        arrived(early + h)
        x = recv[early + h].reshape(n * PIECE, d).astype(jnp.float32)
        y = along_rows(x, [bias_ref.at[1]] * (x.shape[0] // GROUP))
        for p in range(planes):
            y1_late[p] = y[:, p * LANES : (p + 1) * LANES]

        def frame_of(i, c):
            third(h, i)
            return c

        return lax.fori_loop(0, few, frame_of, c)

    lax.fori_loop(0, mine // few, rest, 0)

    for f in range(mine):
        pltpu.make_async_copy(back.at[f, 0], out_ref.at[f], own_sem.at[f]).wait()
    for sem, buffer in ((short_sem.at[2], send_short), (send_sem, send.at[1:]), (back_sem, back)):
        pltpu.make_async_copy(
            buffer.at[:, 0 : n - 1], buffer.at[:, 0 : n - 1], sem
        ).wait()
    total = (n - 1) * mine
    pltpu.make_async_copy(out_ref.at[0:total], out_ref.at[0:total], out_sem).wait()


def kernel_body(sizes, video, norm_gain, qkv_weight, out_weight):
    frames, rows, cols, n, cores = sizes
    d = video.shape[-1]
    tokens = frames * cols
    planes = d // LANES
    mine = frames // n
    chunks = cols * mine // PIECE
    dma = pltpu.SemaphoreType.DMA
    result = pl.pallas_call(
        functools.partial(kernel, sizes),
        out_shape=jax.ShapeDtypeStruct((frames, cols, d), jnp.bfloat16),
        in_specs=[pl.BlockSpec(memory_space=pltpu.HBM)] * 4,
        out_specs=pl.BlockSpec(memory_space=pl.ANY),
        scratch_shapes=[
            pltpu.VMEM((4, 2 * GROUP, GROUP), jnp.float32),
            pltpu.VMEM(norm_gain.shape, jnp.float32),
            pltpu.VMEM((tokens, d), jnp.bfloat16),
            pltpu.VMEM(qkv_weight.shape, jnp.bfloat16),
            pltpu.VMEM(out_weight.shape, jnp.bfloat16),
            pltpu.VMEM((planes, tokens, LANES), jnp.float32),
            pltpu.VMEM((planes, n * PIECE, LANES), jnp.float32),
            pltpu.VMEM((planes, tokens // 2, LANES), jnp.float32),
            pltpu.VMEM((2, n, PIECE, d // 2), jnp.bfloat16),
            pltpu.VMEM((2, cores, n // cores, PIECE, d // 2), jnp.bfloat16),
            pltpu.VMEM((chunks, n, PIECE, d), jnp.bfloat16),
            pltpu.VMEM((chunks, cores, n // cores, PIECE, d), jnp.bfloat16),
            pltpu.VMEM((planes, tokens // 2, LANES), jnp.float32),
            pltpu.VMEM((planes, n * PIECE, LANES), jnp.float32),
            pltpu.VMEM((mine, n, cols, d), jnp.bfloat16),
            dma((2,)),
            dma((3, 2)),
            dma((3,)),
            dma,
            dma((chunks,)),
            dma,
            dma,
            dma((mine,)),
        ],
        compiler_params=pltpu.CompilerParams(
            collective_id=0, has_side_effects=True, vmem_limit_bytes=52 * 1024 * 1024
        ),
        cost_estimate=pl.CostEstimate(
            flops=2 * tokens * d * 4 * d * 3, bytes_accessed=8 * tokens * d, transcendentals=0
        ),
    )(norm_gain, video.reshape(tokens, d), qkv_weight, out_weight)
    return result.reshape(video.shape)


def fits(frames, rows, cols, n, cores, d):
    if frames % n or n != rows * cores or n % 2 or d % (2 * HEAD_DIM):
        return False
    mine = frames // n
    if PIECE % mine or cols != PIECE or GROUP % frames or rows * PIECE != GROUP:
        return False
    half = cols // 2
    if half % (PIECE // mine) or mine % (PIECE // half):
        return False
    if PIECE // mine % 2 or n * PIECE != 2 * GROUP or rows * cores * cols != 2 * GROUP or d % (2 * LANES):
        return False
    return GROUP % (cores * cols) == 0 and (n * PIECE) % GROUP == 0


def solution(mesh):
    def body(video, norm_gain, qkv_weight, out_weight):
        frames, here, cols, d = video.shape
        cores = mesh.shape["ba"]
        rows = here * mesh.shape["aa"]
        n = mesh.shape["aa"] * cores
        if here == 1 and fits(frames, rows, cols, n, cores, d):
            sizes = (frames, rows, cols, n, cores)
            return kernel_body(sizes, video, norm_gain, qkv_weight, out_weight)
        return general_body(video, norm_gain, qkv_weight, out_weight)

    return jax.shard_map(
        body,
        mesh=mesh,
        in_specs=(P("groups", "aa", "ba", None), P(), P(), P()),
        out_specs=P("groups", "aa", "ba", None),
        check_vma=False,
    )
```
